32 devices in a mesh: batch: 16 (over z, x, core), tm: 2 (over y).
Axes of the slice: x: 2, y: 2, z: 4, core: 2. Of those that a mesh axis runs over, the one named last changes fastest.
Arguments:
- audio: bfloat16 [64, 256, 768], P('batch', 'tm'), as said below
- video: bfloat16 [64, 128, 1024], P('batch'), as said below
- pair_ids: int32 [64], P('batch'), may hold values from 0 to 63, each once
- windows: int32 [64], P('batch'), may hold values from 1 to 32, as said below
- lengths: int32 [64], P('batch'), may hold values from 64 to 256, as said below
- w_qkv: bfloat16 [768, 2304], replicated, as said below
- w_out: bfloat16 [768, 768], replicated, may hold values from -0.21875 to 0.21875
- w_query: bfloat16 [1024, 768], replicated, may hold values from -0.1875 to 0.1875
- w_audio_embed: bfloat16 [768, 768], replicated, may hold values from -0.21875 to 0.21875
- w_video_embed: bfloat16 [768, 768], replicated, may hold values from -0.21875 to 0.21875
Outputs:
- audio_mixed: bfloat16 [64, 256, 768], P('batch', 'tm')
- audio_embed: float32 [64, 768], P('batch')
- video_embed: float32 [64, 768], P('batch')
- logits: float32 [64, 64], P('batch')
- row_loss: float32 [64], P('batch')
The draws below stay inside these ranges and needn't reach their ends.
Inputs may be any that keep to these rules, and one draw needn't show every extreme that they name: `pair_ids`: a permutation of the clip numbers. `windows`: some clip reaches 32 in every draw. `lengths`: some clip is valid over all 256 frames in every draw. `audio`: frame features. `video`: token features. `w_qkv`: projection weights of scale 768 to the minus one half.
All inputs are finite; a program needn't handle non-finite values.
Results may differ from the reference program's by a relative error of at most 0.0065.
Values may be sent and summed in bfloat16 or wider, within the bound.
No kernel may reach another device: no remote copies, remote signals or barrier semaphores. Data moves between devices by JAX's collectives and lax.ppermute only.
A program may use at most 128 MiB of HBM per device.

```python
import jax
import jax.numpy as jnp
from jax import lax

HA = 12
HS = 64
DV = 1024
E = 768
FD = 128
VT = 128
DA = 768
WMAX = 32
CLIPS = 64
FRAMES = 256


def draw_audio(key, part):
    key_list = jax.random.split(key, 1)
    shape = (CLIPS, FRAMES, DA)
    return jax.random.normal(key_list[0], shape, jnp.float32).astype(jnp.bfloat16)


def draw_video(key, part):
    key_list = jax.random.split(key, 1)
    shape = (CLIPS, VT, DV)
    return jax.random.normal(key_list[0], shape, jnp.float32).astype(jnp.bfloat16)


def draw_w_qkv(key, part):
    key_list = jax.random.split(key, 3)
    factor = DA ** (-0.5)
    first_block = jax.random.normal(key_list[0], (DA, DA), jnp.float32) * factor
    second_block = jax.random.normal(key_list[1], (DA, DA), jnp.float32) * factor
    third_block = jax.random.normal(key_list[2], (DA, DA), jnp.float32) * factor
    return jnp.concatenate([first_block, second_block, third_block], axis=1).astype(jnp.bfloat16)


def draw_windows(key, part):
    key_one, key_two = jax.random.split(key, 2)
    drawn = jax.random.randint(key_one, (CLIPS,), 1, WMAX + 1)
    widest = jax.random.randint(key_two, (), 0, CLIPS)
    return jnp.where(jnp.arange(CLIPS, dtype=jnp.int32) == widest, WMAX, drawn).astype(jnp.int32)


def draw_lengths(key, part):
    key_one, key_two = jax.random.split(jax.random.fold_in(key, 7), 2)
    drawn = jax.random.randint(key_one, (CLIPS,), FRAMES // 4, FRAMES + 1)
    fullest = jax.random.randint(key_two, (), 0, CLIPS)
    return jnp.where(jnp.arange(CLIPS, dtype=jnp.int32) == fullest, FRAMES, drawn).astype(jnp.int32)


def bell_draw(key, shape, spread, bound, held_as=jnp.bfloat16):
    entries = jax.random.normal(key, shape, jnp.float32) * spread
    return jnp.minimum(jnp.maximum(entries, -bound), bound).astype(held_as)


def setup_inputs(seed: int = 0) -> dict:
    seeds = jax.random.split(jax.random.key(seed), 11)
    audio = draw_audio(jax.random.fold_in(seeds[10], 71), 0)
    video = draw_video(jax.random.fold_in(seeds[10], 71), 0)
    pair_ids = jax.random.permutation(seeds[2], CLIPS).astype(jnp.int32)
    windows = draw_windows(jax.random.fold_in(seeds[10], 71), 0)
    lengths = draw_lengths(jax.random.fold_in(seeds[10], 71), 0)
    w_qkv = draw_w_qkv(jax.random.fold_in(seeds[10], 71), 0)
    w_out = bell_draw(seeds[6], (DA, DA), DA ** -0.5, 0.21875)
    w_query = bell_draw(seeds[7], (DV, DA), DV ** -0.5, 0.1875)
    w_audio_embed = bell_draw(seeds[8], (DA, E), DA ** -0.5, 0.21875)
    w_video_embed = bell_draw(seeds[9], (DA, E), DA ** -0.5, 0.21875)
    return {"audio": audio, "video": video, "pair_ids": pair_ids, "windows": windows, "lengths": lengths, "w_qkv": w_qkv, "w_out": w_out, "w_query": w_query, "w_audio_embed": w_audio_embed, "w_video_embed": w_video_embed}


NEG_LARGE = -1e+30
LOGIT_SCALE = 10.0
LOGIT_BIAS = -10.0

def kept_bf16(array):
    return lax.optimization_barrier(array.astype(jnp.bfloat16)).astype(jnp.float32)

def softmax_parts(scores, allowed):
    scores = jnp.where(allowed, scores, NEG_LARGE)
    highest = lax.optimization_barrier(jnp.max(scores, axis=-1, keepdims=True))
    weights = jnp.where(allowed, jnp.exp(scores - highest), 0.0)
    return (weights, lax.optimization_barrier(jnp.sum(weights, axis=-1)))

def unit_rows(matrix):
    return matrix / jnp.sqrt(lax.optimization_barrier(jnp.sum(matrix * matrix, axis=1, keepdims=True)) + 1e-06)

def reference(audio, video, pair_ids, windows, lengths, w_qkv, w_out, w_query, w_audio_embed, w_video_embed):
    head_scale = HS ** (-0.5)
    blocks = FRAMES // FD
    key_span = FD + 2 * WMAX
    starts = jnp.arange(blocks, dtype=jnp.int32) * FD
    gather_index = starts[:, None] + jnp.arange(key_span, dtype=jnp.int32)[None, :]
    query_pos = starts[:, None] + jnp.arange(FD, dtype=jnp.int32)[None, :]
    key_pos = gather_index - WMAX
    distance = jnp.abs(query_pos[:, :, None] - key_pos[:, None, :])
    inside = ((key_pos >= 0) & (key_pos < FRAMES))[:, None, :]
    frame_index = jnp.arange(FRAMES, dtype=jnp.int32)

    def one_clip(packed):
        audio_clip, video_clip, window, length = packed
        projected = kept_bf16(jnp.dot(audio_clip, w_qkv, preferred_element_type=jnp.float32))
        queries = projected[:, :DA].reshape(blocks, FD, HA, HS)
        keys_all = projected[:, DA:2 * DA]
        values_all = projected[:, 2 * DA:]
        key_blocks = jnp.pad(keys_all, ((WMAX, WMAX), (0, 0)))[gather_index].reshape(blocks, key_span, HA, HS)
        value_blocks = jnp.pad(values_all, ((WMAX, WMAX), (0, 0)))[gather_index].reshape(blocks, key_span, HA, HS)
        allowed = (distance <= window) & inside & ((key_pos[:, None, :] < length) | (distance == 0))
        scores = jnp.einsum('bqhd,bkhd->bhqk', queries, key_blocks) * head_scale
        weights, totals = softmax_parts(scores, allowed[:, None])
        context = jnp.einsum('bhqk,bkhd->bqhd', kept_bf16(weights), value_blocks)
        context = context / jnp.transpose(totals, (0, 2, 1))[..., None]
        context = context.astype(jnp.bfloat16).reshape(FRAMES, DA)
        mixed_rows = (audio_clip.astype(jnp.float32) + jnp.dot(context, w_out, preferred_element_type=jnp.float32)).astype(jnp.bfloat16)
        asking = kept_bf16(jnp.dot(video_clip, w_query, preferred_element_type=jnp.float32)).reshape(VT, HA, HS)
        in_clip = frame_index < length
        cross_scores = jnp.einsum('qhd,khd->hqk', asking, keys_all.reshape(FRAMES, HA, HS)) * head_scale
        cross_weights, cross_totals = softmax_parts(cross_scores, in_clip[None, None, :])
        heard_ctx = jnp.einsum('hqk,khd->qhd', kept_bf16(cross_weights), values_all.reshape(FRAMES, HA, HS))
        heard_ctx = heard_ctx / jnp.transpose(cross_totals)[..., None]
        video_pool = lax.optimization_barrier(jnp.mean(heard_ctx, axis=0)).reshape(DA).astype(jnp.bfloat16)
        frame_sum = lax.optimization_barrier(jnp.sum(jnp.where(in_clip[:, None], mixed_rows.astype(jnp.float32), 0.0), axis=0))
        audio_pool = (frame_sum / length.astype(jnp.float32)).astype(jnp.bfloat16)
        return (mixed_rows, audio_pool, video_pool)
    audio_mixed, audio_pool, video_pool = lax.map(one_clip, (audio, video, windows, lengths))
    audio_embed = unit_rows(jnp.dot(audio_pool, w_audio_embed, preferred_element_type=jnp.float32))
    video_embed = unit_rows(jnp.dot(video_pool, w_video_embed, preferred_element_type=jnp.float32))
    logits = LOGIT_SCALE * jnp.dot(audio_embed, video_embed.T, precision=lax.Precision.HIGHEST) + LOGIT_BIAS
    columns = jnp.arange(CLIPS, dtype=jnp.int32)
    pair_signs = jnp.where(columns[None, :] == pair_ids[:, None], 1.0, -1.0)
    row_loss = lax.optimization_barrier(jnp.sum(jnp.logaddexp(0.0, -pair_signs * logits), axis=1))
    return (audio_mixed, audio_embed, video_embed, logits, row_loss)
```

```python
import functools

import jax
import jax.numpy as jnp
from jax import lax
from jax.experimental import pallas as pl
from jax.experimental.pallas import tpu as pltpu
from jax.sharding import PartitionSpec as P

HA = 12
HS = 64
NEG_LARGE = -1e30
LOGIT_SCALE = 10.0
LOGIT_BIAS = -10.0
F32 = jnp.float32
BF16 = jnp.bfloat16
LANES = 128
STAT_ROWS = 16
NT = (((1,), (1,)), ((), ()))
VMEM = pltpu.VMEM
MIB = 1 << 20


def whole(count):
    return [pl.BlockSpec(memory_space=VMEM)] * count


def params(mib):
    return pltpu.CompilerParams(vmem_limit_bytes=mib * MIB)


def cost(flops, moved, exps=0):
    return pl.CostEstimate(flops=flops, bytes_accessed=moved, transcendentals=exps)


def dot_f32(a, b):
    return jnp.dot(a, b, preferred_element_type=F32)


def dot_nt(a, b):
    return lax.dot_general(a, b, NT, preferred_element_type=F32)


def split_heads(rows, scale):
    lane = lax.broadcasted_iota(jnp.int32, (1, LANES), 1)
    low = jnp.where(lane < HS, scale, 0.0).astype(BF16)
    high = jnp.where(lane < HS, 0.0, scale).astype(BF16)
    return jnp.concatenate([rows * low, rows * high], axis=0)


def front_kernel(
    two_sided, lengths, audio_in, video_in, w_qkv, w_query, w_out, w_audio, w_video,
    stats, weights, keys, audio, halo, wq, wk, wv, wout, waudio, wvideo,
    ask_w, video, asking, sems,
):
    clips, frames, width = audio.shape
    tokens = video.shape[1]
    side = halo.shape[2]
    tm = lax.axis_index("tm")
    pairs = [
        (audio_in, audio),
        (w_qkv.at[:, width : 2 * width], wk),
        (w_query, ask_w),
        (video_in, video),
        (w_qkv.at[:, 2 * width : 3 * width], wv),
        (w_qkv.at[:, 0:width], wq),
        (w_out, wout),
        (w_audio, waudio),
        (w_video, wvideo),
    ]
    if two_sided:
        pairs.append((audio_in.at[:, frames - side : frames, :], halo.at[0]))
        pairs.append((audio_in.at[:, 0:side, :], halo.at[1]))
    else:
        start = pl.multiple_of((1 - tm) * (frames - side), side)
        pairs.append((audio_in.at[:, pl.ds(start, side), :], halo.at[0]))
    copies = [pltpu.make_async_copy(src, dst, sems.at[i]) for i, (src, dst) in enumerate(pairs)]
    for copy in copies:
        copy.start()
    copies[0].wait()
    copies[1].wait()
    chunk = 2 * LANES
    flat = audio[...].reshape(clips * frames, width)
    for at in range(0, width, chunk):
        part = dot_f32(flat, wk[:, at : at + chunk]).astype(BF16)
        keys[:, :, at : at + chunk] = part.reshape(clips, frames, chunk)
    copies[2].wait()
    copies[3].wait()
    flat_video = video[...].reshape(clips * tokens, video.shape[2])
    for at in range(0, width, chunk):
        part = dot_f32(flat_video, ask_w[:, at : at + chunk]).astype(BF16)
        asking[:, :, at : at + chunk] = part.reshape(clips, tokens, chunk)

    def one_clip(c, carry):
        place = tm * frames + lax.broadcasted_iota(jnp.int32, (frames, 1), 0)
        valid = place < lengths[c]
        for pair in range(HA // 2):
            cols = slice(pair * LANES, (pair + 1) * LANES)
            both = split_heads(asking[c, :, cols], HS**-0.5)
            scores = jnp.where(valid, dot_nt(keys[c, :, cols], both), NEG_LARGE)
            peak = jnp.max(scores, axis=0, keepdims=True)
            rising = jnp.exp(scores - peak)
            total = jnp.sum(rising, axis=0, keepdims=True)
            weights[c, :, pair * 2 * tokens : (pair + 1) * 2 * tokens] = rising.astype(BF16)
            for k in range(2):
                row = 2 * pair + k
                stats[0, c, row : row + 1, :] = peak[:, k * tokens : (k + 1) * tokens]
                stats[1, c, row : row + 1, :] = total[:, k * tokens : (k + 1) * tokens]
        rest = (STAT_ROWS - HA, tokens)
        stats[0, c, HA:STAT_ROWS, :] = jnp.zeros(rest, F32)
        stats[1, c, HA:STAT_ROWS, :] = jnp.ones(rest, F32)
        return carry

    lax.fori_loop(0, clips, one_clip, 0)
    for copy in copies[4:]:
        copy.wait()


def front(lengths, audio, video, w_qkv, w_query, w_out, w_audio, w_video, two_sided):
    clips, frames, width = audio.shape
    tokens, depth = video.shape[1:]
    side = frames // 4
    square = VMEM((width, width), BF16)
    copies = 11 if two_sided else 10
    return pl.pallas_call(
        functools.partial(front_kernel, two_sided),
        name="front",
        out_shape=[
            VMEM((2, clips, STAT_ROWS, tokens), F32),
            VMEM((clips, frames, HA * tokens), BF16),
            VMEM((clips, frames, width), BF16),
            VMEM((clips, frames, width), BF16),
            VMEM((copies - 9, clips, side, width), BF16),
        ]
        + [square] * 6,
        in_specs=[pl.BlockSpec(memory_space=pltpu.SMEM)] + [pl.BlockSpec(memory_space=pl.ANY)] * 7,
        out_specs=whole(11),
        scratch_shapes=[
            VMEM((depth, width), BF16),
            VMEM((clips, tokens, depth), BF16),
            VMEM((clips, tokens, width), BF16),
            pltpu.SemaphoreType.DMA((copies,)),
        ],
        compiler_params=params(24),
        cost_estimate=cost(2_000_000_000, 12_000_000, 800_000),
    )(lengths, audio, video, w_qkv, w_query, w_out, w_audio, w_video)


def project_kernel(audio, wq, wv, queries, values):
    clips, frames, width = audio.shape
    chunk = 2 * LANES
    flat = audio[...].reshape(clips * frames, width)
    for weight, out in ((wv, values), (wq, queries)):
        for at in range(0, width, chunk):
            part = dot_f32(flat, weight[:, at : at + chunk]).astype(BF16)
            out[:, :, at : at + chunk] = part.reshape(clips, frames, chunk)


def project(audio, wq, wv):
    out = VMEM(audio.shape, BF16)
    return pl.pallas_call(
        project_kernel,
        name="project",
        out_shape=[out, out],
        in_specs=whole(3),
        out_specs=whole(2),
        compiler_params=params(16),
        cost_estimate=cost(1_200_000_000, 5_000_000),
    )(audio, wq, wv)


def pool_kernel(stats, others, weights, values, wvideo, out, pooled):
    clips, frames, width = values.shape
    tokens = stats.shape[3]
    core = lax.rem(lax.axis_index("batch"), 2)
    peak = stats[0]
    for k in range(others.shape[0]):
        peak = jnp.maximum(peak, others[k, 0])
    mine = jnp.exp(stats[0] - peak)
    total = stats[1] * mine
    for k in range(others.shape[0]):
        total = total + others[k, 1] * jnp.exp(others[k, 0] - peak)
    alpha = mine / (total * tokens)
    head = lax.broadcasted_iota(jnp.int32, (STAT_ROWS, tokens), 0)
    owner = lax.broadcasted_iota(jnp.int32, (STAT_ROWS, width), 0)
    lane_head = lax.broadcasted_iota(jnp.int32, (STAT_ROWS, width), 1) // HS
    pooled[...] = jnp.zeros(pooled.shape, F32)
    for c in range(clips):
        spread = jnp.concatenate(
            [jnp.where(head == h, alpha[c], 0.0).astype(BF16) for h in range(HA)], axis=1
        )
        share = dot_nt(spread, weights[c])
        high = share.astype(BF16)
        low = (share - high.astype(F32)).astype(BF16)
        heard = dot_f32(jnp.concatenate([high, low], axis=0), values[c])
        heard = heard[:STAT_ROWS] + heard[STAT_ROWS:]
        row = jnp.sum(jnp.where(owner == lane_head, heard, 0.0), axis=0, keepdims=True)
        pooled[pl.ds(core * clips + c, 1), :] = row
    rows = pooled[...]
    high = rows.astype(BF16)
    low = (rows - high.astype(F32)).astype(BF16)
    both = dot_f32(jnp.concatenate([high, low], axis=0), wvideo[...])
    out[...] = both[: 2 * clips] + both[2 * clips :]


def pool(stats, others, weights, values, wvideo):
    clips, frames, width = values.shape
    return pl.pallas_call(
        pool_kernel,
        name="pool",
        out_shape=VMEM((2 * clips, wvideo.shape[1]), F32),
        in_specs=whole(5),
        out_specs=pl.BlockSpec(memory_space=VMEM),
        scratch_shapes=[VMEM((2 * clips, width), F32)],
        compiler_params=params(16),
        cost_estimate=cost(200_000_000, 2_000_000),
    )(stats, others, weights, values, wvideo)


def attend(two_sided, c, windows, lengths, queries, keys, values, near_k, near_v, ext_k, ext_v, context, to):
    clips, frames, width = queries.shape
    side = frames // 4
    block = 2 * side
    span = 4 * side
    tm = lax.axis_index("tm")
    for own, near, ext in ((keys, near_k, ext_k), (values, near_v, ext_v)):
        if two_sided:
            ext[0:side, :] = near[0, c]
            ext[side : side + frames, :] = own[c]
            ext[side + frames : 2 * side + frames, :] = near[1, c]
        else:
            ext[pl.ds(pl.multiple_of(tm * side, side), frames), :] = own[c]
            ext[pl.ds(pl.multiple_of((1 - tm) * frames, side), side), :] = near[0, c]
    first = tm * frames - side if two_sided else tm * (frames - side)
    last = lax.axis_size("tm") * frames
    lane = lax.broadcasted_iota(jnp.int32, (block, LANES), 1)
    ones = jnp.ones((span, LANES), BF16)
    for b in range(frames // block):
        at = b * block if two_sided else b * side
        key_pos = first + at + lax.broadcasted_iota(jnp.int32, (block, span), 1)
        query_pos = tm * frames + b * block + lax.broadcasted_iota(jnp.int32, (block, span), 0)
        distance = jnp.abs(query_pos - key_pos)
        allowed = (distance <= windows[c]) & ((key_pos < lengths[c]) | (distance == 0))
        if two_sided:
            allowed = allowed & (key_pos >= 0) & (key_pos < last)
        allowed = jnp.concatenate([allowed, allowed], axis=0)
        for pair in range(HA // 2):
            cols = slice(pair * LANES, (pair + 1) * LANES)
            both = split_heads(queries[c, b * block : (b + 1) * block, cols], HS**-0.5)
            scores = jnp.where(allowed, dot_nt(both, ext_k[at : at + span, cols]), NEG_LARGE)
            rising = jnp.exp(scores - jnp.max(scores, axis=1, keepdims=True)).astype(BF16)
            mix = dot_f32(rising, jnp.concatenate([ext_v[at : at + span, cols], ones], axis=1))
            top = jnp.where(lane < HS, mix[:block, :LANES], mix[block:, :LANES])
            total = jnp.where(lane < HS, mix[:block, LANES:], mix[block:, LANES:])
            context[to, b * block : (b + 1) * block, cols] = (top / total).astype(BF16)


def window_first_kernel(
    two_sided, done, windows, lengths, queries, keys, values, near, wk, wv,
    context, near_k, near_v, ext_k, ext_v,
):
    sides, clips, side, width = near.shape
    flat = near[...].reshape(sides * clips * side, width)
    chunk = 2 * LANES
    for weight, out in ((wk, near_k), (wv, near_v)):
        for at in range(0, width, chunk):
            part = dot_f32(flat, weight[:, at : at + chunk]).astype(BF16)
            out[:, :, :, at : at + chunk] = part.reshape(sides, clips, side, chunk)

    def one_clip(c, carry):
        attend(two_sided, c, windows, lengths, queries, keys, values, near_k, near_v, ext_k, ext_v, context, c)
        return carry

    lax.fori_loop(0, done, one_clip, 0)


def ext_scratch(frames, width, two_sided):
    rows = frames + (frames // 4) * (2 if two_sided else 1)
    return [VMEM((rows, width), BF16)] * 2


def window_first(done, windows, lengths, queries, keys, values, near, wk, wv, two_sided):
    clips, frames, width = queries.shape
    smem = pl.BlockSpec(memory_space=pltpu.SMEM)
    return pl.pallas_call(
        functools.partial(window_first_kernel, two_sided, done),
        name="window_first",
        out_shape=[VMEM((done, frames, width), BF16), VMEM(near.shape, BF16), VMEM(near.shape, BF16)],
        in_specs=[smem, smem] + whole(6),
        out_specs=whole(3),
        scratch_shapes=ext_scratch(frames, width, two_sided),
        compiler_params=params(16),
        cost_estimate=cost(1_000_000_000, 5_000_000, 400_000),
    )(windows, lengths, queries, keys, values, near, wk, wv)


def window_last_kernel(
    two_sided, done, windows, lengths, queries, keys, values, near_k, near_v, before, audio, wout,
    mixed, frame_sum, context, ext_k, ext_v,
):
    clips, frames, width = queries.shape
    context[0:done] = before[...]

    def one_clip(c, carry):
        attend(two_sided, c, windows, lengths, queries, keys, values, near_k, near_v, ext_k, ext_v, context, c)
        return carry

    lax.fori_loop(done, clips, one_clip, 0)
    place = lax.axis_index("tm") * frames + lax.broadcasted_iota(jnp.int32, (frames, 1), 0)
    flat = context[...].reshape(clips * frames, width)
    chunk = 2 * LANES
    for at in range(0, width, chunk):
        cols = slice(at, at + chunk)
        part = dot_f32(flat, wout[:, cols]).reshape(clips, frames, chunk)
        part = (audio[:, :, cols].astype(F32) + part).astype(BF16)
        mixed[:, :, cols] = part
        for c in range(clips):
            kept = jnp.where(place < lengths[c], part[c].astype(F32), 0.0)
            frame_sum[c : c + 1, cols] = jnp.sum(kept, axis=0, keepdims=True)


def window_last(done, windows, lengths, queries, keys, values, near_k, near_v, before, audio, wout, two_sided):
    clips, frames, width = queries.shape
    smem = pl.BlockSpec(memory_space=pltpu.SMEM)
    return pl.pallas_call(
        functools.partial(window_last_kernel, two_sided, done),
        name="window_last",
        out_shape=[jax.ShapeDtypeStruct(audio.shape, BF16), VMEM((clips, width), F32)],
        in_specs=[smem, smem] + whole(8),
        out_specs=whole(2),
        scratch_shapes=[VMEM((clips, frames, width), BF16)] + ext_scratch(frames, width, two_sided),
        compiler_params=params(16),
        cost_estimate=cost(1_000_000_000, 5_000_000, 400_000),
    )(windows, lengths, queries, keys, values, near_k, near_v, before, audio, wout)


def unit_rows(matrix):
    return matrix / jnp.sqrt(jnp.sum(matrix * matrix, axis=1, keepdims=True) + 1e-06)


def audio_head_kernel(lengths, mine, other, waudio, out):
    clips = mine.shape[0]
    row = lax.broadcasted_iota(jnp.int32, (clips, 1), 0)
    count = jnp.zeros((clips, 1), F32)
    for c in range(clips):
        count = jnp.where(row == c, lengths[c].astype(F32), count)
    mean = ((mine[...] + other[...]) / count).astype(BF16)
    out[...] = unit_rows(dot_f32(mean, waudio[...]))


def audio_head(lengths, mine, other, waudio):
    return pl.pallas_call(
        audio_head_kernel,
        name="audio_head",
        out_shape=jax.ShapeDtypeStruct((mine.shape[0], waudio.shape[1]), F32),
        in_specs=[pl.BlockSpec(memory_space=pltpu.SMEM)] + whole(3),
        out_specs=pl.BlockSpec(memory_space=VMEM),
        compiler_params=params(8),
        cost_estimate=cost(20_000_000, 1_200_000),
    )(lengths, mine, other, waudio)


def logits_kernel(masks, pair_ids, audio, kept, received, logits, row_loss, video_embed, units):
    clips = audio.shape[0]
    place = lax.axis_index("batch")
    core = lax.rem(place, 2)
    chip = lax.div(place, 2)
    chosen = jnp.where(core == 1, kept[...].astype(F32), received[...].astype(F32))
    chosen = unit_rows(chosen)
    rows = 2 * clips
    for j, mask in enumerate(masks):
        at = pl.multiple_of((chip ^ mask) * rows, rows)
        units[pl.ds(at, rows), :] = chosen[j * rows : (j + 1) * rows]
    own = units[pl.ds(pl.multiple_of(chip * rows, rows), rows), :]
    video_embed[...] = jnp.where(core == 0, own[:clips], own[clips:])
    found = LOGIT_SCALE * lax.dot_general(
        audio[...], units[...], NT, precision=lax.Precision.HIGHEST, preferred_element_type=F32
    )
    found = found + LOGIT_BIAS
    logits[...] = found
    column = lax.broadcasted_iota(jnp.int32, found.shape, 1)
    row = lax.broadcasted_iota(jnp.int32, found.shape, 0)
    wanted = jnp.zeros(found.shape, jnp.int32)
    for c in range(clips):
        wanted = jnp.where(row == c, pair_ids[c], wanted)
    signed = jnp.where(column == wanted, -found, found)
    loss = jnp.maximum(signed, 0.0) + jnp.log1p(jnp.exp(-jnp.abs(signed)))
    loss = jnp.sum(loss, axis=1, keepdims=True)
    square = lax.broadcasted_iota(jnp.int32, (clips, clips), 0) == lax.broadcasted_iota(
        jnp.int32, (clips, clips), 1
    )
    row_loss[...] = jnp.sum(jnp.where(square, loss, 0.0), axis=0, keepdims=True)


def logits_and_loss(masks, pair_ids, audio, kept, received):
    clips, width = audio.shape
    total = kept.shape[0]
    return pl.pallas_call(
        functools.partial(logits_kernel, masks),
        name="logits_and_loss",
        out_shape=[
            jax.ShapeDtypeStruct((clips, total), F32),
            jax.ShapeDtypeStruct((1, clips), F32),
            jax.ShapeDtypeStruct((clips, width), F32),
        ],
        in_specs=[pl.BlockSpec(memory_space=pltpu.SMEM)] + whole(3),
        out_specs=whole(3),
        scratch_shapes=[VMEM((total, width), F32)],
        compiler_params=params(8),
        cost_estimate=cost(20_000_000, 300_000),
    )(pair_ids, audio, kept, received)


def others_on_tm(x):
    count = lax.axis_size("tm")
    moved = [
        lax.ppermute(x, "tm", [(i, (i + shift) % count) for i in range(count)])
        for shift in range(1, count)
    ]
    return jnp.stack(moved)


def swap_tm(x, cores):
    batch = lax.axis_size("batch")
    pairs = [(2 * b + t, 2 * b + 1 - t) for b in range(batch) if b % 2 in cores for t in range(2)]
    return lax.ppermute(x, ("batch", "tm"), pairs)


def gather_video(mine):
    batch = lax.axis_size("batch")
    tm = lax.axis_size("tm")

    def among_cores(x, source):
        return lax.ppermute(x, "batch", [(b, b ^ 1) for b in range(batch) if b % 2 == source])

    def among_chips(x, mask):
        return lax.ppermute(x, "batch", [(b, b ^ (2 * mask)) for b in range(batch) if b % 2 == 1])

    mine = mine + among_cores(mine, 0)
    if tm == 2:
        mine = mine + swap_tm(mine, (1,))
    else:
        mine = lax.psum(mine, "tm")
    held = mine.astype(BF16)
    masks = [0]
    chips = batch // 2
    top = chips
    while top > 1:
        step = 4 if top % 4 == 0 else 2
        top //= step
        moves = [k * top for k in range(1, step)]
        held = jnp.concatenate([held] + [among_chips(held, move) for move in moves], axis=0)
        masks = masks + [mask ^ move for move in moves for mask in masks]
    return held, among_cores(held, 1), masks


def per_device(
    audio, video, pair_ids, windows, lengths, w_qkv, w_out, w_query, w_audio_embed, w_video_embed
):
    clips = audio.shape[0]
    tm = lax.axis_size("tm")
    two_sided = tm > 2
    stats, weights, keys, held_audio, halo, wq, wk, wv, wout, waudio, wvideo = front(
        lengths, audio, video, w_qkv, w_query, w_out, w_audio_embed, w_video_embed, two_sided
    )
    others = others_on_tm(stats)
    if two_sided:
        near = jnp.stack(
            [
                lax.ppermute(halo[0], "tm", [(i, i + 1) for i in range(tm - 1)]),
                lax.ppermute(halo[1], "tm", [(i + 1, i) for i in range(tm - 1)]),
            ]
        )
    else:
        near = swap_tm(halo, (0, 1))
    queries, values = project(held_audio, wq, wv)
    video_part = pool(stats, others, weights, values, wvideo)
    kept, received, masks = gather_video(video_part)
    done = clips // 2
    context, near_k, near_v = window_first(
        done, windows, lengths, queries, keys, values, near, wk, wv, two_sided
    )
    audio_mixed, frame_sum = window_last(
        done, windows, lengths, queries, keys, values, near_k, near_v, context, held_audio, wout, two_sided
    )
    if two_sided:
        frame_sum = lax.psum(frame_sum, "tm")
        other_sum = jnp.zeros_like(frame_sum)
    else:
        other_sum = swap_tm(frame_sum, (0, 1))
    audio_embed = audio_head(lengths, frame_sum, other_sum, waudio)
    logits, row_loss, video_embed = logits_and_loss(masks, pair_ids, audio_embed, kept, received)
    return (audio_mixed, audio_embed, video_embed, logits, row_loss.reshape(clips))


def solution(mesh):
    in_specs = (
        P("batch", "tm", None),
        P("batch", None, None),
        P("batch"),
        P("batch"),
        P("batch"),
        P(),
        P(),
        P(),
        P(),
        P(),
    )
    out_specs = (
        P("batch", "tm", None),
        P("batch", None),
        P("batch", None),
        P("batch", None),
        P("batch"),
    )
    return jax.shard_map(
        per_device, mesh=mesh, in_specs=in_specs, out_specs=out_specs, check_vma=False
    )
```

```python
import functools

import jax
import jax.numpy as jnp
from jax import lax
from jax.experimental import pallas as pl
from jax.experimental.pallas import tpu as pltpu
from jax.sharding import PartitionSpec as P

HA = 12
HS = 64
NEG_LARGE = -1e30
LOGIT_SCALE = 10.0
LOGIT_BIAS = -10.0
F32 = jnp.float32
BF16 = jnp.bfloat16
LANES = 128
STAT_ROWS = 16
NT = (((1,), (1,)), ((), ()))
VMEM = pltpu.VMEM
MIB = 1 << 20


def whole(count):
    return [pl.BlockSpec(memory_space=VMEM)] * count


def params(mib):
    return pltpu.CompilerParams(vmem_limit_bytes=mib * MIB)


def cost(flops, moved, exps=0):
    return pl.CostEstimate(flops=flops, bytes_accessed=moved, transcendentals=exps)


def dot_f32(a, b):
    return jnp.dot(a, b, preferred_element_type=F32)


def dot_nt(a, b):
    return lax.dot_general(a, b, NT, preferred_element_type=F32)


def split_heads(rows, scale):
    lane = lax.broadcasted_iota(jnp.int32, (1, LANES), 1)
    low = jnp.where(lane < HS, scale, 0.0).astype(BF16)
    high = jnp.where(lane < HS, 0.0, scale).astype(BF16)
    return jnp.concatenate([rows * low, rows * high], axis=0)


def load_all(pairs, sems):
    copies = [pltpu.make_async_copy(src, dst, sems.at[i]) for i, (src, dst) in enumerate(pairs)]
    for copy in copies:
        copy.start()
    return copies


def front_kernel(
    two_sided, lengths, windows, pair_ids, audio_in, video_in, w_qkv, w_query,
    peaks, spans, info, weights, keys, audio, halo, wq, wk, wv,
    small, ask_w, video, asking, totals, sems,
):
    clips, frames, width = audio.shape
    tokens = video.shape[1]
    side = halo.shape[2]
    tm = lax.axis_index("tm")
    pairs = [
        (lengths, small.at[0]),
        (windows, small.at[1]),
        (pair_ids, small.at[2]),
        (audio_in, audio),
        (w_qkv.at[:, width : 2 * width], wk),
        (video_in, video),
        (w_query, ask_w),
        (w_qkv.at[:, 2 * width : 3 * width], wv),
        (w_qkv.at[:, 0:width], wq),
    ]
    if two_sided:
        pairs.append((audio_in.at[:, frames - side : frames, :], halo.at[0]))
        pairs.append((audio_in.at[:, 0:side, :], halo.at[1]))
    else:
        start = pl.multiple_of((1 - tm) * (frames - side), side)
        pairs.append((audio_in.at[:, pl.ds(start, side), :], halo.at[0]))
    copies = load_all(pairs, sems)
    for copy in copies[:5]:
        copy.wait()
    for k in range(3):
        for c in range(clips):
            info[k, c] = jnp.full(info.shape[2:], small[k, c], jnp.int32)
    chunk = 2 * LANES
    flat = audio[...].reshape(clips * frames, width)
    for at in range(0, width, chunk):
        part = dot_f32(flat, wk[:, at : at + chunk]).astype(BF16)
        keys[:, :, at : at + chunk] = part.reshape(clips, frames, chunk)
    copies[5].wait()
    copies[6].wait()
    flat_video = video[...].reshape(clips * tokens, video.shape[2])
    for at in range(0, width, chunk):
        part = dot_f32(flat_video, ask_w[:, at : at + chunk]).astype(BF16)
        asking[:, :, at : at + chunk] = part.reshape(clips, tokens, chunk)
    place = tm * frames + lax.broadcasted_iota(jnp.int32, (frames, 1), 0)
    columns = [slice(pair * LANES, (pair + 1) * LANES) for pair in range(HA // 2)]
    for c in range(clips):
        valid = place < small[0, c]
        scores = [
            dot_nt(keys[c, :, cols], split_heads(asking[c, :, cols], HS**-0.5)) for cols in columns
        ]
        scores = [jnp.where(valid, s, NEG_LARGE) for s in scores]
        highest = [jnp.max(s, axis=0, keepdims=True) for s in scores]
        rising = [jnp.exp(s - peak) for s, peak in zip(scores, highest)]
        sums = [jnp.sum(r, axis=0, keepdims=True) for r in rising]
        for pair in range(HA // 2):
            weights[c, :, pair * 2 * tokens : (pair + 1) * 2 * tokens] = rising[pair].astype(BF16)
            for k in range(2):
                row = slice(2 * pair + k, 2 * pair + k + 1)
                peaks[c, row, :] = highest[pair][:, k * tokens : (k + 1) * tokens]
                totals[c, row, :] = sums[pair][:, k * tokens : (k + 1) * tokens]
        rest = (STAT_ROWS - HA, tokens)
        peaks[c, HA:STAT_ROWS, :] = jnp.zeros(rest, F32)
        totals[c, HA:STAT_ROWS, :] = jnp.ones(rest, F32)
    spans[...] = peaks[...] + jnp.log(totals[...])
    for copy in copies[7:]:
        copy.wait()


def in_hbm(*arrays):
    return [pltpu.with_memory_space_constraint(x, pltpu.HBM) for x in arrays]


def from_hbm(count):
    return [pl.BlockSpec(memory_space=pltpu.HBM)] * count


def front(lengths, windows, pair_ids, audio, video, w_qkv, w_query, two_sided):
    clips, frames, width = audio.shape
    tokens, depth = video.shape[1:]
    side = frames // 4
    square = VMEM((width, width), BF16)
    sides = 2 if two_sided else 1
    stat = VMEM((clips, STAT_ROWS, tokens), F32)
    return pl.pallas_call(
        functools.partial(front_kernel, two_sided),
        name="front",
        out_shape=[
            stat,
            stat,
            VMEM((3, clips, 8, LANES), jnp.int32),
            VMEM((clips, frames, HA * tokens), BF16),
            VMEM((clips, frames, width), BF16),
            VMEM((clips, frames, width), BF16),
            VMEM((sides, clips, side, width), BF16),
            square,
            square,
            square,
        ],
        in_specs=from_hbm(7),
        out_specs=whole(10),
        scratch_shapes=[
            pltpu.SMEM((3, clips), jnp.int32),
            VMEM((depth, width), BF16),
            VMEM((clips, tokens, depth), BF16),
            VMEM((clips, tokens, width), BF16),
            stat,
            pltpu.SemaphoreType.DMA((9 + sides,)),
        ],
        compiler_params=params(24),
        cost_estimate=cost(2_000_000_000, 8_000_000, 800_000),
    )(*in_hbm(lengths, windows, pair_ids, audio, video, w_qkv, w_query))


def attend(two_sided, tasks, info, queries, keys, values, near_k, near_v, ext_k, ext_v, out):
    clips, frames, width = queries.shape
    side = frames // 4
    block = 2 * side
    span = 4 * side
    tm = lax.axis_index("tm")
    last = lax.axis_size("tm") * frames
    lane = lax.broadcasted_iota(jnp.int32, (block, LANES), 1)
    ones = jnp.ones((span, LANES), BF16)
    columns = [slice(pair * LANES, (pair + 1) * LANES) for pair in range(HA // 2)]
    for i, (c, half) in enumerate(tasks):
        if half == "inner":
            b = tm
            key, value, first = keys.at[c], values.at[c], tm * frames
        else:
            b = 1 - tm if half == "outer" else half
            way = 0 if half == "outer" else half
            key, value = ext_k.at[i % 2], ext_v.at[i % 2]
            first = tm * frames + b * block - side
            for own, near, ext in ((keys, near_k, key), (values, near_v, value)):
                if half == "outer":
                    ext[pl.ds(pl.multiple_of(tm * side, side), 3 * side), :] = own[
                        c, pl.ds(pl.multiple_of((1 - tm) * side, side), 3 * side), :
                    ]
                    ext[pl.ds(pl.multiple_of((1 - tm) * 3 * side, side), side), :] = near[way, c]
                else:
                    ext[(1 - b) * side : (1 - b) * side + 3 * side, :] = own[c, b * side : b * side + 3 * side, :]
                    ext[b * 3 * side : b * 3 * side + side, :] = near[way, c]
        key_pos = first + lax.broadcasted_iota(jnp.int32, (block, span), 1)
        query_pos = tm * frames + b * block + lax.broadcasted_iota(jnp.int32, (block, span), 0)
        distance = jnp.abs(query_pos - key_pos)
        length, window = info[0, c, 0:1, :], info[1, c, 0:1, :]
        allowed = (distance <= window) & ((key_pos < length) | (distance == 0))
        if two_sided:
            allowed = allowed & (key_pos >= 0) & (key_pos < last)
        allowed = jnp.concatenate([allowed, allowed], axis=0)
        rows = pl.ds(pl.multiple_of(b * block, block), block)
        scores = [
            dot_nt(split_heads(queries[c, rows, cols], HS**-0.5), key[:, cols]) for cols in columns
        ]
        scores = [jnp.where(allowed, s, NEG_LARGE) for s in scores]
        highest = [jnp.max(s, axis=1, keepdims=True) for s in scores]
        rising = [jnp.exp(s - peak).astype(BF16) for s, peak in zip(scores, highest)]
        mixes = [
            dot_f32(r, jnp.concatenate([value[:, cols], ones], axis=1))
            for r, cols in zip(rising, columns)
        ]
        for mix, cols in zip(mixes, columns):
            top = jnp.where(lane < HS, mix[:block, :LANES], mix[block:, :LANES])
            total = jnp.where(lane < HS, mix[:block, LANES:], mix[block:, LANES:])
            out[i, :, cols] = (top / total).astype(BF16)


def project_kernel(
    two_sided, tasks, info, audio, keys, wq, wv, w_out, w_audio, w_video,
    queries, values, wout, waudio, wvideo, done, sems,
):
    clips, frames, width = audio.shape
    copies = load_all([(w_video, wvideo), (w_out, wout), (w_audio, waudio)], sems)
    chunk = 2 * LANES
    flat = audio[...].reshape(clips * frames, width)
    for weight, out in ((wv, values), (wq, queries)):
        for at in range(0, width, chunk):
            part = dot_f32(flat, weight[:, at : at + chunk]).astype(BF16)
            out[:, :, at : at + chunk] = part.reshape(clips, frames, chunk)
    attend(two_sided, tasks, info, queries, keys, values, None, None, None, None, done)
    for copy in copies:
        copy.wait()


def context_of(tasks, frames, width):
    return VMEM((max(len(tasks), 1), frames // 2, width), BF16)


def project(two_sided, tasks, info, audio, keys, wq, wv, w_out, w_audio, w_video):
    clips, frames, width = audio.shape
    out = VMEM(audio.shape, BF16)
    square = VMEM((width, width), BF16)
    return pl.pallas_call(
        functools.partial(project_kernel, two_sided, tasks),
        name="project",
        out_shape=[out, out, square, square, square, context_of(tasks, frames, width)],
        in_specs=whole(5) + from_hbm(3),
        out_specs=whole(6),
        scratch_shapes=[pltpu.SemaphoreType.DMA((3,))],
        compiler_params=params(16),
        cost_estimate=cost(1_200_000_000, 5_000_000),
    )(info, audio, keys, wq, wv, *in_hbm(w_out, w_audio, w_video))


def inner_kernel(two_sided, tasks, info, queries, keys, values, done):
    attend(two_sided, tasks, info, queries, keys, values, None, None, None, None, done)


def inner(two_sided, tasks, info, queries, keys, values):
    clips, frames, width = queries.shape
    return pl.pallas_call(
        functools.partial(inner_kernel, two_sided, tasks),
        name="inner",
        out_shape=context_of(tasks, frames, width),
        in_specs=whole(4),
        out_specs=pl.BlockSpec(memory_space=VMEM),
        compiler_params=params(16),
        cost_estimate=cost(300_000_000, 2_000_000, 100_000),
    )(info, queries, keys, values)


def outer_kernel(
    two_sided, tasks, info, queries, keys, values, near, wk, wv, done, near_k, near_v, ext_k, ext_v
):
    sides, clips, side, width = near.shape
    flat = near[...].reshape(sides * clips * side, width)
    chunk = 2 * LANES
    for weight, out in ((wk, near_k), (wv, near_v)):
        for at in range(0, width, chunk):
            part = dot_f32(flat, weight[:, at : at + chunk]).astype(BF16)
            out[:, :, :, at : at + chunk] = part.reshape(sides, clips, side, chunk)
    attend(two_sided, tasks, info, queries, keys, values, near_k, near_v, ext_k, ext_v, done)


def outer(two_sided, tasks, info, queries, keys, values, near, wk, wv):
    clips, frames, width = queries.shape
    beyond = VMEM(near.shape, BF16)
    return pl.pallas_call(
        functools.partial(outer_kernel, two_sided, tasks),
        name="outer",
        out_shape=[context_of(tasks, frames, width), beyond, beyond],
        in_specs=whole(7),
        out_specs=whole(3),
        scratch_shapes=[VMEM((2, frames, width), BF16)] * 2,
        compiler_params=params(16),
        cost_estimate=cost(1_000_000_000, 5_000_000, 400_000),
    )(info, queries, keys, values, near, wk, wv)


def mix_kernel(
    two_sided, plan, info, queries, keys, values, near_k, near_v, audio, wout, *rest
):
    count = len(plan) - 1
    before = rest[:count]
    mixed, frame_sum, context, done, ext_k, ext_v = rest[count:]
    clips, frames, width = queries.shape
    block = frames // 2
    tm = lax.axis_index("tm")
    attend(two_sided, plan[-1], info, queries, keys, values, near_k, near_v, ext_k, ext_v, done)
    for tasks, held in zip(plan, (*before, done)):
        for i, (c, half) in enumerate(tasks):
            b = tm if half == "inner" else 1 - tm if half == "outer" else half
            context[c, pl.ds(pl.multiple_of(b * block, block), block), :] = held[i]
    place = tm * frames + lax.broadcasted_iota(jnp.int32, (frames, 1), 0)
    flat = context[...].reshape(clips * frames, width)
    chunk = 2 * LANES
    for at in range(0, width, chunk):
        cols = slice(at, at + chunk)
        part = dot_f32(flat, wout[:, cols]).reshape(clips, frames, chunk)
        part = (audio[:, :, cols].astype(F32) + part).astype(BF16)
        mixed[:, :, cols] = part
        for c in range(clips):
            kept = jnp.where(place < info[0, c, 0:1, 0:1], part[c].astype(F32), 0.0)
            frame_sum[c : c + 1, cols] = jnp.sum(kept, axis=0, keepdims=True)


def mix(two_sided, plan, info, queries, keys, values, near_k, near_v, audio, wout, before):
    clips, frames, width = queries.shape
    return pl.pallas_call(
        functools.partial(mix_kernel, two_sided, plan),
        name="mix",
        out_shape=[VMEM(audio.shape, BF16), VMEM((clips, width), F32)],
        in_specs=whole(8 + len(before)),
        out_specs=whole(2),
        scratch_shapes=[VMEM((clips, frames, width), BF16), context_of(plan[-1], frames, width)]
        + [VMEM((2, frames, width), BF16)] * 2,
        compiler_params=params(16),
        cost_estimate=cost(1_000_000_000, 5_000_000, 400_000),
    )(info, queries, keys, values, near_k, near_v, audio, wout, *before)


def pool_kernel(peaks, spans, others, weights, values, wvideo, out):
    clips, frames, width = values.shape
    tokens = peaks.shape[2]
    core = lax.rem(lax.axis_index("batch"), 2)
    top = spans[...]
    for k in range(others.shape[0]):
        top = jnp.maximum(top, others[k])
    total = jnp.exp(spans[...] - top)
    for k in range(others.shape[0]):
        total = total + jnp.exp(others[k] - top)
    alpha = jnp.exp(peaks[...] - top) / (total * tokens)
    head = lax.broadcasted_iota(jnp.int32, (STAT_ROWS, tokens), 0)
    owner = lax.broadcasted_iota(jnp.int32, (STAT_ROWS, width), 0)
    lane_head = lax.broadcasted_iota(jnp.int32, (STAT_ROWS, width), 1) // HS
    spread = [
        jnp.concatenate([jnp.where(head == h, alpha[c], 0.0).astype(BF16) for h in range(HA)], axis=1)
        for c in range(clips)
    ]
    share = [dot_nt(spread[c], weights[c]) for c in range(clips)]
    high = [s.astype(BF16) for s in share]
    low = [(s - h.astype(F32)).astype(BF16) for s, h in zip(share, high)]
    heard = [dot_f32(jnp.concatenate([high[c], low[c]], axis=0), values[c]) for c in range(clips)]
    heard = [h[:STAT_ROWS] + h[STAT_ROWS:] for h in heard]
    pooled = jnp.concatenate(
        [jnp.sum(jnp.where(owner == lane_head, h, 0.0), axis=0, keepdims=True) for h in heard], axis=0
    )
    rows = jnp.concatenate(
        [jnp.where(core == 0, pooled, 0.0), jnp.where(core == 0, 0.0, pooled)], axis=0
    )
    high = rows.astype(BF16)
    low = (rows - high.astype(F32)).astype(BF16)
    both = dot_f32(jnp.concatenate([high, low], axis=0), wvideo[...])
    out[...] = both[: 2 * clips] + both[2 * clips :]


def pool(peaks, spans, others, weights, values, wvideo):
    clips, frames, width = values.shape
    return pl.pallas_call(
        pool_kernel,
        name="pool",
        out_shape=VMEM((2 * clips, wvideo.shape[1]), F32),
        in_specs=whole(6),
        out_specs=pl.BlockSpec(memory_space=VMEM),
        compiler_params=params(16),
        cost_estimate=cost(200_000_000, 2_000_000),
    )(peaks, spans, others, weights, values, wvideo)


def unit_rows(matrix):
    return matrix / jnp.sqrt(jnp.sum(matrix * matrix, axis=1, keepdims=True) + 1e-06)


def column_of(info, k):
    return jnp.concatenate([info[k, c, 0:1, 0:1] for c in range(info.shape[1])], axis=0)


def audio_head_kernel(info, mine, other, waudio, out, held):
    mean = ((mine[...] + other[...]) / column_of(info, 0).astype(F32)).astype(BF16)
    found = unit_rows(dot_f32(mean, waudio[...]))
    out[...] = found
    held[...] = found


def audio_head(info, mine, other, waudio):
    shape = (mine.shape[0], waudio.shape[1])
    return pl.pallas_call(
        audio_head_kernel,
        name="audio_head",
        out_shape=[jax.ShapeDtypeStruct(shape, F32), VMEM(shape, F32)],
        in_specs=whole(4),
        out_specs=whole(2),
        compiler_params=params(8),
        cost_estimate=cost(20_000_000, 1_200_000),
    )(info, mine, other, waudio)


def logits_kernel(masks, info, audio, held, logits, row_loss, video_embed, units):
    clips = audio.shape[0]
    place = lax.axis_index("batch")
    core = lax.rem(place, 2)
    chip = lax.div(place, 2)
    found = unit_rows(held[...].astype(F32))
    rows = 2 * clips
    for j, mask in enumerate(masks):
        at = pl.multiple_of((chip ^ mask) * rows, rows)
        units[pl.ds(at, rows), :] = found[j * rows : (j + 1) * rows]
    video_embed[...] = jnp.where(core == 0, found[:clips], found[clips:rows])
    found = LOGIT_SCALE * lax.dot_general(
        audio[...], units[...], NT, precision=lax.Precision.HIGHEST, preferred_element_type=F32
    )
    found = found + LOGIT_BIAS
    logits[...] = found
    column = lax.broadcasted_iota(jnp.int32, found.shape, 1)
    signed = jnp.where(column == column_of(info, 2), -found, found)
    loss = jnp.maximum(signed, 0.0) + jnp.log1p(jnp.exp(-jnp.abs(signed)))
    loss = jnp.sum(loss, axis=1, keepdims=True)
    square = lax.broadcasted_iota(jnp.int32, (clips, clips), 0) == lax.broadcasted_iota(
        jnp.int32, (clips, clips), 1
    )
    row_loss[...] = jnp.sum(jnp.where(square, loss, 0.0), axis=0, keepdims=True)


def logits_and_loss(masks, info, audio, held):
    clips, width = audio.shape
    total = held.shape[0]
    return pl.pallas_call(
        functools.partial(logits_kernel, masks),
        name="logits_and_loss",
        out_shape=[
            jax.ShapeDtypeStruct((clips, total), F32),
            jax.ShapeDtypeStruct((1, clips), F32),
            jax.ShapeDtypeStruct((clips, width), F32),
        ],
        in_specs=whole(3),
        out_specs=whole(3),
        scratch_shapes=[VMEM((total, width), F32)],
        compiler_params=params(8),
        cost_estimate=cost(20_000_000, 300_000),
    )(info, audio, held)


def others_on_tm(x):
    count = lax.axis_size("tm")
    return jnp.stack(
        [
            lax.ppermute(x, "tm", [(i, (i + shift) % count) for i in range(count)])
            for shift in range(1, count)
        ]
    )


def beside(send, operand, work, inputs):
    operand, inputs = lax.optimization_barrier((operand, inputs))
    moved = send(operand)
    return lax.optimization_barrier((moved, work(*inputs)))


def move(x, mask, flip=0):
    batch = lax.axis_size("batch")
    tm = lax.axis_size("tm")
    pairs = [(b * tm + t, (b ^ mask) * tm + (t ^ flip)) for b in range(batch) for t in range(tm)]
    return lax.ppermute(x, ("batch", "tm"), pairs)


def per_device(
    audio, video, pair_ids, windows, lengths, w_qkv, w_out, w_query, w_audio_embed, w_video_embed
):
    clips = audio.shape[0]
    tm = lax.axis_size("tm")
    chips = lax.axis_size("batch") // 2
    two_sided = tm > 2
    if two_sided:
        plan = ((), (), tuple((c, 0) for c in range(clips)), tuple((c, 1) for c in range(clips)))
    else:
        inside = tuple((c, "inner") for c in range(clips))
        outside = tuple((c, "outer") for c in range(clips))
        cut = clips // 2
        plan = (inside[:1], inside[1:2], inside[2:] + outside[:cut], outside[cut:])
    peaks, spans, info, weights, keys, held_audio, halo, wq, wk, wv = front(
        lengths, windows, pair_ids, audio, video, w_qkv, w_query, two_sided
    )
    others = others_on_tm(spans)
    if two_sided:
        near = jnp.stack(
            [
                lax.ppermute(halo[0], "tm", [(i, i + 1) for i in range(tm - 1)]),
                lax.ppermute(halo[1], "tm", [(i + 1, i) for i in range(tm - 1)]),
            ]
        )
    else:
        near = move(halo, 0, 1)
    queries, values, wout, waudio, wvideo, part_a = project(
        two_sided, plan[0], info, held_audio, keys, wq, wv, w_out, w_audio_embed, w_video_embed
    )
    found = pool(peaks, spans, others, weights, values, wvideo)
    local = (info, queries, keys, values)
    if plan[1]:
        moved, part_b = beside(
            lambda x: move(x, 1), found, lambda *held: inner(two_sided, plan[1], *held), local
        )
    else:
        moved, part_b = move(found, 1), part_a
    found = found + moved

    def share(x):
        return lax.psum(x, "tm") if two_sided else x + move(x, 0, 1)

    found, (part_c, near_k, near_v) = beside(
        share, found, lambda *held: outer(two_sided, plan[2], *held), (*local, near, wk, wv)
    )
    held = found.astype(BF16)
    masks = [0]
    top = chips // 2
    moved, (audio_mixed, frame_sum) = beside(
        lambda x: move(x, 2 * top + 1),
        held,
        lambda *held: mix(two_sided, plan, *held[:8], held[8:]),
        (*local, near_k, near_v, held_audio, wout, part_a, part_b, part_c),
    )
    held = jnp.concatenate([held, moved], axis=0)
    masks = masks + [top]
    other_sum = None
    while top > 1:
        step = 4 if top % 4 == 0 else 2
        top //= step
        moves = [k * top for k in range(1, step)]
        held = jnp.concatenate([held] + [move(held, 2 * m + 1) for m in moves], axis=0)
        masks = masks + [mask ^ m for m in moves for mask in masks]
    if two_sided:
        frame_sum = lax.psum(frame_sum, "tm")
        other_sum = jnp.zeros_like(frame_sum)
    else:
        other_sum = move(frame_sum, 0, 1)
    audio_embed, unit_audio = audio_head(info, frame_sum, other_sum, waudio)
    logits, row_loss, video_embed = logits_and_loss(masks, info, unit_audio, held)
    return (audio_mixed, audio_embed, video_embed, logits, row_loss.reshape(clips))


def solution(mesh):
    in_specs = (
        P("batch", "tm", None),
        P("batch", None, None),
        P("batch"),
        P("batch"),
        P("batch"),
        P(),
        P(),
        P(),
        P(),
        P(),
    )
    out_specs = (
        P("batch", "tm", None),
        P("batch", None),
        P("batch", None),
        P("batch", None),
        P("batch"),
    )
    return jax.shard_map(
        per_device, mesh=mesh, in_specs=in_specs, out_specs=out_specs, check_vma=False
    )
```

```python
import functools

import jax
import jax.numpy as jnp
from jax import lax
from jax.experimental import pallas as pl
from jax.experimental.pallas import tpu as pltpu
from jax.sharding import PartitionSpec as P

HA = 12
HS = 64
NEG_LARGE = -1e30
LOGIT_SCALE = 10.0
LOGIT_BIAS = -10.0
F32 = jnp.float32
BF16 = jnp.bfloat16
LANES = 128
STAT_ROWS = 16
NT = (((1,), (1,)), ((), ()))
VMEM = pltpu.VMEM
MIB = 1 << 20


def whole(count):
    return [pl.BlockSpec(memory_space=VMEM)] * count


def params(mib):
    return pltpu.CompilerParams(vmem_limit_bytes=mib * MIB)


def cost(flops, moved, exps=0):
    return pl.CostEstimate(flops=flops, bytes_accessed=moved, transcendentals=exps)


def dot_f32(a, b):
    return jnp.dot(a, b, preferred_element_type=F32)


def dot_nt(a, b):
    return lax.dot_general(a, b, NT, preferred_element_type=F32)


def split_heads(rows, scale):
    lane = lax.broadcasted_iota(jnp.int32, (1, LANES), 1)
    low = jnp.where(lane < HS, scale, 0.0).astype(BF16)
    high = jnp.where(lane < HS, 0.0, scale).astype(BF16)
    return jnp.concatenate([rows * low, rows * high], axis=0)


class Pieces:
    def __init__(self, src, dst, sem, pieces):
        rows = dst.shape[0] // pieces
        cuts = [pl.ds(k * rows, rows) for k in range(pieces)]
        self.copies = [pltpu.make_async_copy(src.at[cut], dst.at[cut], sem) for cut in cuts]

    def start(self):
        for copy in self.copies:
            copy.start()

    def wait(self):
        for copy in self.copies:
            copy.wait()


def load_all(pairs, sems):
    copies = [Pieces(src, dst, sems.at[i], pieces) for i, (src, dst, pieces) in enumerate(pairs)]
    for copy in copies:
        copy.start()
    return copies


def in_hbm(*arrays):
    return [pltpu.with_memory_space_constraint(x, pltpu.HBM) for x in arrays]


def from_hbm(count):
    return [pl.BlockSpec(memory_space=pltpu.HBM)] * count


def front_kernel(
    two_sided, lengths, windows, pair_ids, audio_in, video_in, w_qkv, w_query,
    peaks, spans, info, weights, keys, audio, halo, wq, wk, wv,
    small, ask_w, video, asking, totals, sems,
):
    clips, frames, width = audio.shape
    tokens = video.shape[1]
    side = halo.shape[2]
    chunk = 2 * LANES
    cuts = [slice(at, at + chunk) for at in range(0, width, chunk)]
    count = iter(range(sems.shape[0]))

    def piece(src, dst, pieces=1):
        return Pieces(src, dst, sems.at[next(count)], pieces)

    def start(copies):
        for copy in copies:
            copy.start()

    def wait(copies):
        for copy in copies:
            copy.wait()

    ints = [piece(src, small.at[k]) for k, src in enumerate((lengths, windows, pair_ids))]
    of_audio = piece(audio_in, audio, 2)
    of_keys = [piece(w_qkv.at[:, width : 2 * width], wk, 2)]
    of_video = piece(video_in, video, 2)
    of_asking = [piece(w_query, ask_w, 2)]
    later = [piece(w_qkv.at[:, 2 * width : 3 * width], wv, 2), piece(w_qkv.at[:, 0:width], wq, 2)]
    if two_sided:
        later.append(piece(audio_in.at[:, frames - side : frames, :], halo.at[0]))
        later.append(piece(audio_in.at[:, 0:side, :], halo.at[1]))
    else:
        at = pl.multiple_of((1 - lax.axis_index("tm")) * (frames - side), side)
        later.append(piece(audio_in.at[:, pl.ds(at, side), :], halo.at[0]))

    def make_keys():
        of_audio.wait()
        flat = audio[...].reshape(clips * frames, width)
        wait(of_keys)
        for cut in cuts:
            keys[:, :, cut] = dot_f32(flat, wk[:, cut]).astype(BF16).reshape(clips, frames, chunk)

    def make_asking():
        of_video.wait()
        flat = video[...].reshape(clips * tokens, video.shape[2])
        wait(of_asking)
        for cut in cuts:
            asking[:, :, cut] = dot_f32(flat, ask_w[:, cut]).astype(BF16).reshape(clips, tokens, chunk)

    start(ints + [of_audio] + of_keys)
    wait(ints)
    start([of_video] + of_asking)
    make_keys()
    start(later)
    make_asking()
    for k in range(3):
        for c in range(clips):
            info[k, c] = jnp.full(info.shape[2:], small[k, c], jnp.int32)
    place = lax.axis_index("tm") * frames + lax.broadcasted_iota(jnp.int32, (frames, 1), 0)
    columns = [slice(pair * LANES, (pair + 1) * LANES) for pair in range(HA // 2)]
    for c in range(clips):
        valid = place < small[0, c]
        scores = [
            dot_nt(keys[c, :, cols], split_heads(asking[c, :, cols], HS**-0.5)) for cols in columns
        ]
        scores = [jnp.where(valid, s, NEG_LARGE) for s in scores]
        highest = [jnp.max(s, axis=0, keepdims=True) for s in scores]
        rising = [jnp.exp(s - peak) for s, peak in zip(scores, highest)]
        sums = [jnp.sum(r, axis=0, keepdims=True) for r in rising]
        for pair in range(HA // 2):
            weights[c, :, pair * 2 * tokens : (pair + 1) * 2 * tokens] = rising[pair].astype(BF16)
            for k in range(2):
                row = slice(2 * pair + k, 2 * pair + k + 1)
                peaks[c, row, :] = highest[pair][:, k * tokens : (k + 1) * tokens]
                totals[c, row, :] = sums[pair][:, k * tokens : (k + 1) * tokens]
        rest = (STAT_ROWS - HA, tokens)
        peaks[c, HA:STAT_ROWS, :] = jnp.zeros(rest, F32)
        totals[c, HA:STAT_ROWS, :] = jnp.ones(rest, F32)
    spans[...] = peaks[...] + jnp.log(totals[...])
    wait(later)


def front(lengths, windows, pair_ids, audio, video, w_qkv, w_query, two_sided):
    clips, frames, width = audio.shape
    tokens, depth = video.shape[1:]
    square = VMEM((width, width), BF16)
    sides = 2 if two_sided else 1
    stat = VMEM((clips, STAT_ROWS, tokens), F32)
    return pl.pallas_call(
        functools.partial(front_kernel, two_sided),
        name="front",
        out_shape=[
            stat,
            stat,
            VMEM((3, clips, 8, LANES), jnp.int32),
            VMEM((clips, frames, HA * tokens), BF16),
            VMEM((clips, frames, width), BF16),
            VMEM((clips, frames, width), BF16),
            VMEM((sides, clips, frames // 4, width), BF16),
            square,
            square,
            square,
        ],
        in_specs=from_hbm(7),
        out_specs=whole(10),
        scratch_shapes=[
            pltpu.SMEM((3, clips), jnp.int32),
            VMEM((depth, width), BF16),
            VMEM((clips, tokens, depth), BF16),
            VMEM((clips, tokens, width), BF16),
            stat,
            pltpu.SemaphoreType.DMA((7 + sides + 2 * (width // (2 * LANES)),)),
        ],
        compiler_params=params(24),
        cost_estimate=cost(2_000_000_000, 8_000_000, 800_000),
    )(*in_hbm(lengths, windows, pair_ids, audio, video, w_qkv, w_query))


def attend(two_sided, tasks, info, queries, keys, values, near_k, near_v, ext_k, ext_v, out):
    clips, frames, width = queries.shape
    side = frames // 4
    block = 2 * side
    span = 4 * side
    tm = lax.axis_index("tm")
    last = lax.axis_size("tm") * frames
    lane = lax.broadcasted_iota(jnp.int32, (block, LANES), 1)
    ones = jnp.ones((span, LANES), BF16)
    columns = [slice(pair * LANES, (pair + 1) * LANES) for pair in range(HA // 2)]
    for i, (c, half) in enumerate(tasks):
        if half == "inner":
            b = tm
            key, value, first = keys.at[c], values.at[c], tm * frames
        else:
            b = 1 - tm if half == "outer" else half
            way = 0 if half == "outer" else half
            key, value = ext_k.at[i % 2], ext_v.at[i % 2]
            first = tm * frames + b * block - side
            for own, near, ext in ((keys, near_k, key), (values, near_v, value)):
                if half == "outer":
                    ext[pl.ds(pl.multiple_of(tm * side, side), 3 * side), :] = own[
                        c, pl.ds(pl.multiple_of((1 - tm) * side, side), 3 * side), :
                    ]
                    ext[pl.ds(pl.multiple_of((1 - tm) * 3 * side, side), side), :] = near[way, c]
                else:
                    ext[(1 - b) * side : (1 - b) * side + 3 * side, :] = own[c, b * side : b * side + 3 * side, :]
                    ext[b * 3 * side : b * 3 * side + side, :] = near[way, c]
        key_pos = first + lax.broadcasted_iota(jnp.int32, (block, span), 1)
        query_pos = tm * frames + b * block + lax.broadcasted_iota(jnp.int32, (block, span), 0)
        distance = jnp.abs(query_pos - key_pos)
        length, window = info[0, c, 0:1, :], info[1, c, 0:1, :]
        allowed = (distance <= window) & ((key_pos < length) | (distance == 0))
        if two_sided:
            allowed = allowed & (key_pos >= 0) & (key_pos < last)
        allowed = jnp.concatenate([allowed, allowed], axis=0)
        rows = pl.ds(pl.multiple_of(b * block, block), block)
        scores = [
            dot_nt(split_heads(queries[c, rows, cols], HS**-0.5), key[:, cols]) for cols in columns
        ]
        scores = [jnp.where(allowed, s, NEG_LARGE) for s in scores]
        highest = [jnp.max(s, axis=1, keepdims=True) for s in scores]
        rising = [jnp.exp(s - peak).astype(BF16) for s, peak in zip(scores, highest)]
        mixes = [
            dot_f32(r, jnp.concatenate([value[:, cols], ones], axis=1))
            for r, cols in zip(rising, columns)
        ]
        for mix, cols in zip(mixes, columns):
            top = jnp.where(lane < HS, mix[:block, :LANES], mix[block:, :LANES])
            total = jnp.where(lane < HS, mix[:block, LANES:], mix[block:, LANES:])
            out[i, :, cols] = (top / total).astype(BF16)


def project(flat, weight, out):
    clips, frames, width = out.shape
    chunk = 2 * LANES
    for at in range(0, width, chunk):
        part = dot_f32(flat, weight[:, at : at + chunk]).astype(BF16)
        out[:, :, at : at + chunk] = part.reshape(clips, frames, chunk)


def values_kernel(audio, wv, values):
    clips, frames, width = audio.shape
    project(audio[...].reshape(clips * frames, width), wv, values)


def make_values(audio, wv):
    return pl.pallas_call(
        values_kernel,
        name="values",
        out_shape=VMEM(audio.shape, BF16),
        in_specs=whole(2),
        out_specs=pl.BlockSpec(memory_space=VMEM),
        compiler_params=params(16),
        cost_estimate=cost(600_000_000, 2_000_000),
    )(audio, wv)


def queries_kernel(two_sided, tasks, info, audio, keys, values, wq, queries, done):
    clips, frames, width = audio.shape
    project(audio[...].reshape(clips * frames, width), wq, queries)
    attend(two_sided, tasks, info, queries, keys, values, None, None, None, None, done)


def context_of(tasks, frames, width):
    return VMEM((max(len(tasks), 1), frames // 2, width), BF16)


def make_queries(two_sided, tasks, info, audio, keys, values, wq):
    clips, frames, width = audio.shape
    return pl.pallas_call(
        functools.partial(queries_kernel, two_sided, tasks),
        name="queries",
        out_shape=[VMEM(audio.shape, BF16), context_of(tasks, frames, width)],
        in_specs=whole(5),
        out_specs=whole(2),
        compiler_params=params(16),
        cost_estimate=cost(80_000_000_000, 3_000_000, 100_000),
    )(info, audio, keys, values, wq)


def inner_kernel(two_sided, tasks, info, queries, keys, values, done):
    attend(two_sided, tasks, info, queries, keys, values, None, None, None, None, done)


def inner(two_sided, tasks, info, queries, keys, values):
    clips, frames, width = queries.shape
    return pl.pallas_call(
        functools.partial(inner_kernel, two_sided, tasks),
        name="inner",
        out_shape=context_of(tasks, frames, width),
        in_specs=whole(4),
        out_specs=pl.BlockSpec(memory_space=VMEM),
        compiler_params=params(16),
        cost_estimate=cost(300_000_000, 2_000_000, 100_000),
    )(info, queries, keys, values)


def outer_kernel(
    two_sided, tasks, info, queries, keys, values, near, wk, wv, done, near_k, near_v, ext_k, ext_v
):
    sides, clips, side, width = near.shape
    flat = near[...].reshape(sides * clips * side, width)
    chunk = 2 * LANES
    for weight, out in ((wk, near_k), (wv, near_v)):
        for at in range(0, width, chunk):
            part = dot_f32(flat, weight[:, at : at + chunk]).astype(BF16)
            out[:, :, :, at : at + chunk] = part.reshape(sides, clips, side, chunk)
    attend(two_sided, tasks, info, queries, keys, values, near_k, near_v, ext_k, ext_v, done)


def outer(two_sided, tasks, info, queries, keys, values, near, wk, wv):
    clips, frames, width = queries.shape
    beyond = VMEM(near.shape, BF16)
    return pl.pallas_call(
        functools.partial(outer_kernel, two_sided, tasks),
        name="outer",
        out_shape=[context_of(tasks, frames, width), beyond, beyond],
        in_specs=whole(7),
        out_specs=whole(3),
        scratch_shapes=[VMEM((2, frames, width), BF16)] * 2,
        compiler_params=params(16),
        cost_estimate=cost(1_000_000_000, 5_000_000, 400_000),
    )(info, queries, keys, values, near, wk, wv)


def mix_kernel(
    two_sided, plan, info, queries, keys, values, near_k, near_v, audio, wout, *rest
):
    count = len(plan) - 1
    before = rest[:count]
    mixed, frame_sum, context, done, ext_k, ext_v = rest[count:]
    clips, frames, width = queries.shape
    block = frames // 2
    tm = lax.axis_index("tm")
    attend(two_sided, plan[-1], info, queries, keys, values, near_k, near_v, ext_k, ext_v, done)
    for tasks, held in zip(plan, (*before, done)):
        for i, (c, half) in enumerate(tasks):
            b = tm if half == "inner" else 1 - tm if half == "outer" else half
            context[c, pl.ds(pl.multiple_of(b * block, block), block), :] = held[i]
    place = tm * frames + lax.broadcasted_iota(jnp.int32, (frames, 1), 0)
    flat = context[...].reshape(clips * frames, width)
    chunk = 2 * LANES
    for at in range(0, width, chunk):
        cols = slice(at, at + chunk)
        part = dot_f32(flat, wout[:, cols]).reshape(clips, frames, chunk)
        part = (audio[:, :, cols].astype(F32) + part).astype(BF16)
        mixed[:, :, cols] = part
        for c in range(clips):
            kept = jnp.where(place < info[0, c, 0:1, 0:1], part[c].astype(F32), 0.0)
            frame_sum[c : c + 1, cols] = jnp.sum(kept, axis=0, keepdims=True)


def mix(two_sided, plan, info, queries, keys, values, near_k, near_v, audio, wout, before):
    clips, frames, width = queries.shape
    return pl.pallas_call(
        functools.partial(mix_kernel, two_sided, plan),
        name="mix",
        out_shape=[VMEM(audio.shape, BF16), VMEM((clips, width), F32)],
        in_specs=whole(8 + len(before)),
        out_specs=whole(2),
        scratch_shapes=[VMEM((clips, frames, width), BF16), context_of(plan[-1], frames, width)]
        + [VMEM((2, frames, width), BF16)] * 2,
        compiler_params=params(16),
        cost_estimate=cost(1_000_000_000, 5_000_000, 400_000),
    )(info, queries, keys, values, near_k, near_v, audio, wout, *before)


def pool_kernel(peaks, spans, others, weights, values, wvideo, out):
    clips, frames, width = values.shape
    tokens = peaks.shape[2]
    core = lax.rem(lax.axis_index("batch"), 2)
    top = spans[...]
    for k in range(others.shape[0]):
        top = jnp.maximum(top, others[k])
    total = jnp.exp(spans[...] - top)
    for k in range(others.shape[0]):
        total = total + jnp.exp(others[k] - top)
    alpha = jnp.exp(peaks[...] - top) / (total * tokens)
    head = lax.broadcasted_iota(jnp.int32, (STAT_ROWS, tokens), 0)
    owner = lax.broadcasted_iota(jnp.int32, (STAT_ROWS, width), 0)
    lane_head = lax.broadcasted_iota(jnp.int32, (STAT_ROWS, width), 1) // HS
    spread = [
        jnp.concatenate([jnp.where(head == h, alpha[c], 0.0).astype(BF16) for h in range(HA)], axis=1)
        for c in range(clips)
    ]
    share = [dot_nt(spread[c], weights[c]) for c in range(clips)]
    high = [s.astype(BF16) for s in share]
    low = [(s - h.astype(F32)).astype(BF16) for s, h in zip(share, high)]
    heard = [dot_f32(jnp.concatenate([high[c], low[c]], axis=0), values[c]) for c in range(clips)]
    heard = [h[:STAT_ROWS] + h[STAT_ROWS:] for h in heard]
    pooled = jnp.concatenate(
        [jnp.sum(jnp.where(owner == lane_head, h, 0.0), axis=0, keepdims=True) for h in heard], axis=0
    )
    rows = jnp.concatenate(
        [jnp.where(core == 0, pooled, 0.0), jnp.where(core == 0, 0.0, pooled)], axis=0
    )
    high = rows.astype(BF16)
    low = (rows - high.astype(F32)).astype(BF16)
    both = dot_f32(jnp.concatenate([high, low], axis=0), wvideo[...])
    out[...] = both[: 2 * clips] + both[2 * clips :]


def pool(peaks, spans, others, weights, values, wvideo):
    clips, frames, width = values.shape
    return pl.pallas_call(
        pool_kernel,
        name="pool",
        out_shape=VMEM((2 * clips, wvideo.shape[1]), F32),
        in_specs=whole(6),
        out_specs=pl.BlockSpec(memory_space=VMEM),
        compiler_params=params(16),
        cost_estimate=cost(200_000_000, 2_000_000),
    )(peaks, spans, others, weights, values, wvideo)


def unit_rows(matrix):
    return matrix / jnp.sqrt(jnp.sum(matrix * matrix, axis=1, keepdims=True) + 1e-06)


def column_of(info, k):
    return jnp.concatenate([info[k, c, 0:1, 0:1] for c in range(info.shape[1])], axis=0)


def audio_head_kernel(info, mine, other, waudio, out, held):
    mean = ((mine[...] + other[...]) / column_of(info, 0).astype(F32)).astype(BF16)
    found = unit_rows(dot_f32(mean, waudio[...]))
    out[...] = found
    held[...] = found


def audio_head(info, mine, other, waudio):
    shape = (mine.shape[0], waudio.shape[1])
    return pl.pallas_call(
        audio_head_kernel,
        name="audio_head",
        out_shape=[jax.ShapeDtypeStruct(shape, F32), VMEM(shape, F32)],
        in_specs=whole(4),
        out_specs=whole(2),
        compiler_params=params(8),
        cost_estimate=cost(20_000_000, 1_200_000),
    )(info, mine, other, waudio)


def logits_kernel(masks, info, audio, held, logits, row_loss, video_embed, units):
    clips = audio.shape[0]
    place = lax.axis_index("batch")
    core = lax.rem(place, 2)
    chip = lax.div(place, 2)
    found = unit_rows(held[...].astype(F32))
    rows = 2 * clips
    for j, mask in enumerate(masks):
        at = pl.multiple_of((chip ^ mask) * rows, rows)
        units[pl.ds(at, rows), :] = found[j * rows : (j + 1) * rows]
    video_embed[...] = jnp.where(core == 0, found[:clips], found[clips:rows])
    found = LOGIT_SCALE * lax.dot_general(
        audio[...], units[...], NT, precision=lax.Precision.HIGHEST, preferred_element_type=F32
    )
    found = found + LOGIT_BIAS
    logits[...] = found
    column = lax.broadcasted_iota(jnp.int32, found.shape, 1)
    signed = jnp.where(column == column_of(info, 2), -found, found)
    loss = jnp.maximum(signed, 0.0) + jnp.log1p(jnp.exp(-jnp.abs(signed)))
    loss = jnp.sum(loss, axis=1, keepdims=True)
    square = lax.broadcasted_iota(jnp.int32, (clips, clips), 0) == lax.broadcasted_iota(
        jnp.int32, (clips, clips), 1
    )
    row_loss[...] = jnp.sum(jnp.where(square, loss, 0.0), axis=0, keepdims=True)


def logits_and_loss(masks, info, audio, held):
    clips, width = audio.shape
    total = held.shape[0]
    return pl.pallas_call(
        functools.partial(logits_kernel, masks),
        name="logits_and_loss",
        out_shape=[
            jax.ShapeDtypeStruct((clips, total), F32),
            jax.ShapeDtypeStruct((1, clips), F32),
            jax.ShapeDtypeStruct((clips, width), F32),
        ],
        in_specs=whole(3),
        out_specs=whole(3),
        scratch_shapes=[VMEM((total, width), F32)],
        compiler_params=params(8),
        cost_estimate=cost(20_000_000, 300_000),
    )(info, audio, held)


def others_on_tm(x):
    count = lax.axis_size("tm")
    return jnp.stack(
        [
            lax.ppermute(x, "tm", [(i, (i + shift) % count) for i in range(count)])
            for shift in range(1, count)
        ]
    )


def beside(send, operand, work, inputs):
    operand, inputs = lax.optimization_barrier((operand, inputs))
    moved = send(operand)
    return lax.optimization_barrier((moved, work(*inputs)))


def move(x, mask, flip=0):
    batch = lax.axis_size("batch")
    tm = lax.axis_size("tm")
    pairs = [(b * tm + t, (b ^ mask) * tm + (t ^ flip)) for b in range(batch) for t in range(tm)]
    return lax.ppermute(x, ("batch", "tm"), pairs)


def per_device(
    audio, video, pair_ids, windows, lengths, w_qkv, w_out, w_query, w_audio_embed, w_video_embed
):
    clips = audio.shape[0]
    tm = lax.axis_size("tm")
    chips = lax.axis_size("batch") // 2
    two_sided = tm > 2
    if two_sided:
        plan = ((), (), tuple((c, 0) for c in range(clips)), tuple((c, 1) for c in range(clips)))
    else:
        inside = tuple((c, "inner") for c in range(clips))
        outside = tuple((c, "outer") for c in range(clips))
        cut = clips // 2
        plan = (inside[:1], inside[1:2], inside[2:] + outside[:cut], outside[cut:])
    peaks, spans, info, weights, keys, held_audio, halo, wq, wk, wv = front(
        lengths, windows, pair_ids, audio, video, w_qkv, w_query, two_sided
    )

    def spread(halo):
        if not two_sided:
            return move(halo, 0, 1)
        upward = lax.ppermute(halo[0], "tm", [(i, i + 1) for i in range(tm - 1)])
        downward = lax.ppermute(halo[1], "tm", [(i + 1, i) for i in range(tm - 1)])
        return jnp.stack([upward, downward])

    near = spread(halo)
    others = others_on_tm(spans)
    values = make_values(held_audio, wv)
    queries, part_a = make_queries(two_sided, plan[0], info, held_audio, keys, values, wq)
    others, (queries, part_a) = lax.optimization_barrier((others, (queries, part_a)))
    found = pool(peaks, spans, others, weights, values, w_video_embed)
    local = (info, queries, keys, values)
    if plan[1]:
        moved, part_b = beside(
            lambda x: move(x, 1), found, lambda *held: inner(two_sided, plan[1], *held), local
        )
    else:
        moved, part_b = move(found, 1), part_a
    found = found + moved

    def share(x):
        return lax.psum(x, "tm") if two_sided else x + move(x, 1, 1)

    found, (part_c, near_k, near_v) = beside(
        share, found, lambda *held: outer(two_sided, plan[2], *held), (*local, near, wk, wv)
    )
    held = found.astype(BF16)
    masks = [0]
    top = chips // 2
    moved, (audio_mixed, frame_sum) = beside(
        lambda x: move(x, 2 * top + 1),
        held,
        lambda *held: mix(two_sided, plan, *held[:8], held[8:]),
        (*local, near_k, near_v, held_audio, w_out, part_a, part_b, part_c),
    )
    held = jnp.concatenate([held, moved], axis=0)
    masks = masks + [top]
    if two_sided:
        frame_sum = lax.psum(frame_sum, "tm")
        other_sum = jnp.zeros_like(frame_sum)
    else:
        other_sum = move(frame_sum, 0, 1)
    while top > 1:
        step = 4 if top % 4 == 0 else 2
        top //= step
        moves = [k * top for k in range(1, step)]
        held = jnp.concatenate([held] + [move(held, 2 * m + 1) for m in moves], axis=0)
        masks = masks + [mask ^ m for m in moves for mask in masks]
    audio_embed, unit_audio = audio_head(info, frame_sum, other_sum, w_audio_embed)
    logits, row_loss, video_embed = logits_and_loss(masks, info, unit_audio, held)
    return (audio_mixed, audio_embed, video_embed, logits, row_loss.reshape(clips))


def solution(mesh):
    in_specs = (
        P("batch", "tm", None),
        P("batch", None, None),
        P("batch"),
        P("batch"),
        P("batch"),
        P(),
        P(),
        P(),
        P(),
        P(),
    )
    out_specs = (
        P("batch", "tm", None),
        P("batch", None),
        P("batch", None),
        P("batch", None),
        P("batch"),
    )
    return jax.shard_map(
        per_device, mesh=mesh, in_specs=in_specs, out_specs=out_specs, check_vma=False
    )
```

```python
import functools

import jax
import jax.numpy as jnp
from jax import lax
from jax.experimental import pallas as pl
from jax.experimental.pallas import tpu as pltpu
from jax.sharding import PartitionSpec as P

HA = 12
HS = 64
NEG_LARGE = -1e30
LOGIT_SCALE = 10.0
LOGIT_BIAS = -10.0
F32 = jnp.float32
BF16 = jnp.bfloat16
LANES = 128
STAT_ROWS = 16
STAGED = 3
NT = (((1,), (1,)), ((), ()))
VMEM = pltpu.VMEM
MIB = 1 << 20


def whole(count):
    return [pl.BlockSpec(memory_space=VMEM)] * count


def params(mib):
    return pltpu.CompilerParams(vmem_limit_bytes=mib * MIB)


def cost(flops, moved, exps=0):
    return pl.CostEstimate(flops=flops, bytes_accessed=moved, transcendentals=exps)


def dot_f32(a, b):
    return jnp.dot(a, b, preferred_element_type=F32)


def dot_nt(a, b):
    return lax.dot_general(a, b, NT, preferred_element_type=F32)


def split_heads(rows, scale):
    lane = lax.broadcasted_iota(jnp.int32, (1, LANES), 1)
    low = jnp.where(lane < HS, scale, 0.0).astype(BF16)
    high = jnp.where(lane < HS, 0.0, scale).astype(BF16)
    return jnp.concatenate([rows * low, rows * high], axis=0)


class Pieces:
    def __init__(self, src, dst, sem, pieces):
        rows = dst.shape[0] // pieces
        cuts = [pl.ds(k * rows, rows) for k in range(pieces)]
        self.copies = [pltpu.make_async_copy(src.at[cut], dst.at[cut], sem) for cut in cuts]

    def start(self):
        for copy in self.copies:
            copy.start()

    def wait(self):
        for copy in self.copies:
            copy.wait()


def load_all(pairs, sems):
    copies = [Pieces(src, dst, sems.at[i], pieces) for i, (src, dst, pieces) in enumerate(pairs)]
    for copy in copies:
        copy.start()
    return copies


def in_hbm(*arrays):
    return [pltpu.with_memory_space_constraint(x, pltpu.HBM) for x in arrays]


def from_hbm(count):
    return [pl.BlockSpec(memory_space=pltpu.HBM)] * count


def front_kernel(
    two_sided, lengths, windows, pair_ids, audio_in, video_in, w_qkv, w_query,
    peaks, spans, info, weights, keys, audio, halo, wq, wk, wv,
    small, ask_w, video, asking, totals, sems,
):
    clips, frames, width = audio.shape
    tokens = video.shape[1]
    side = halo.shape[2]
    chunk = 2 * LANES
    cuts = [slice(at, at + chunk) for at in range(0, width, chunk)]
    count = iter(range(sems.shape[0]))

    def piece(src, dst, pieces=1):
        return Pieces(src, dst, sems.at[next(count)], pieces)

    def start(copies):
        for copy in copies:
            copy.start()

    def wait(copies):
        for copy in copies:
            copy.wait()

    ints = [piece(src, small.at[k]) for k, src in enumerate((lengths, windows, pair_ids))]
    of_audio = piece(audio_in, audio, 2)
    of_keys = [piece(w_qkv.at[:, width : 2 * width], wk, 2)]
    of_video = piece(video_in, video, 2)
    of_asking = [piece(w_query, ask_w, 2)]
    later = [piece(w_qkv.at[:, 2 * width : 3 * width], wv, 2), piece(w_qkv.at[:, 0:width], wq, 2)]
    if two_sided:
        later.append(piece(audio_in.at[:, frames - side : frames, :], halo.at[0]))
        later.append(piece(audio_in.at[:, 0:side, :], halo.at[1]))
    else:
        at = pl.multiple_of((1 - lax.axis_index("tm")) * (frames - side), side)
        later.append(piece(audio_in.at[:, pl.ds(at, side), :], halo.at[0]))

    def make_keys():
        of_audio.wait()
        flat = audio[...].reshape(clips * frames, width)
        wait(of_keys)
        for cut in cuts:
            keys[:, :, cut] = dot_f32(flat, wk[:, cut]).astype(BF16).reshape(clips, frames, chunk)

    def make_asking():
        of_video.wait()
        flat = video[...].reshape(clips * tokens, video.shape[2])
        wait(of_asking)
        for cut in cuts:
            asking[:, :, cut] = dot_f32(flat, ask_w[:, cut]).astype(BF16).reshape(clips, tokens, chunk)

    start(ints + [of_audio] + of_keys)
    wait(ints)
    start([of_video] + of_asking)
    make_keys()
    start(later)
    make_asking()
    for k in range(3):
        for c in range(clips):
            info[k, c] = jnp.full(info.shape[2:], small[k, c], jnp.int32)
    place = lax.axis_index("tm") * frames + lax.broadcasted_iota(jnp.int32, (frames, 1), 0)
    columns = [slice(pair * LANES, (pair + 1) * LANES) for pair in range(HA // 2)]
    for c in range(clips):
        valid = place < small[0, c]
        scores = [
            dot_nt(keys[c, :, cols], split_heads(asking[c, :, cols], HS**-0.5)) for cols in columns
        ]
        scores = [jnp.where(valid, s, NEG_LARGE) for s in scores]
        highest = [jnp.max(s, axis=0, keepdims=True) for s in scores]
        rising = [jnp.exp(s - peak) for s, peak in zip(scores, highest)]
        sums = [jnp.sum(r, axis=0, keepdims=True) for r in rising]
        for pair in range(HA // 2):
            weights[c, :, pair * 2 * tokens : (pair + 1) * 2 * tokens] = rising[pair].astype(BF16)
            for k in range(2):
                row = slice(2 * pair + k, 2 * pair + k + 1)
                peaks[c, row, :] = highest[pair][:, k * tokens : (k + 1) * tokens]
                totals[c, row, :] = sums[pair][:, k * tokens : (k + 1) * tokens]
        rest = (STAT_ROWS - HA, tokens)
        peaks[c, HA:STAT_ROWS, :] = jnp.zeros(rest, F32)
        totals[c, HA:STAT_ROWS, :] = jnp.ones(rest, F32)
    spans[...] = peaks[...] + jnp.log(totals[...])
    wait(later)


def front(lengths, windows, pair_ids, audio, video, w_qkv, w_query, two_sided):
    clips, frames, width = audio.shape
    tokens, depth = video.shape[1:]
    square = VMEM((width, width), BF16)
    sides = 2 if two_sided else 1
    stat = VMEM((clips, STAT_ROWS, tokens), F32)
    return pl.pallas_call(
        functools.partial(front_kernel, two_sided),
        name="front",
        out_shape=[
            stat,
            stat,
            VMEM((3, clips, 8, LANES), jnp.int32),
            VMEM((clips, frames, HA * tokens), BF16),
            VMEM((clips, frames, width), BF16),
            VMEM((clips, frames, width), BF16),
            VMEM((sides, clips, frames // 4, width), BF16),
            square,
            square,
            square,
        ],
        in_specs=from_hbm(7),
        out_specs=whole(10),
        scratch_shapes=[
            pltpu.SMEM((3, clips), jnp.int32),
            VMEM((depth, width), BF16),
            VMEM((clips, tokens, depth), BF16),
            VMEM((clips, tokens, width), BF16),
            stat,
            pltpu.SemaphoreType.DMA((7 + sides + 2 * (width // (2 * LANES)),)),
        ],
        compiler_params=params(24),
        cost_estimate=cost(2_000_000_000, 8_000_000, 800_000),
    )(*in_hbm(lengths, windows, pair_ids, audio, video, w_qkv, w_query))


def attend(two_sided, tasks, info, queries, keys, values, near_k, near_v, ext_k, ext_v, out):
    clips, frames, width = queries.shape
    side = frames // 4
    block = 2 * side
    span = 4 * side
    tm = lax.axis_index("tm")
    last = lax.axis_size("tm") * frames
    lane = lax.broadcasted_iota(jnp.int32, (block, LANES), 1)
    ones = jnp.ones((span, LANES), BF16)
    columns = [slice(pair * LANES, (pair + 1) * LANES) for pair in range(HA // 2)]
    units = []
    for i, (c, half) in enumerate(tasks):
        if half == "inner":
            b = tm
            key, value, first = keys.at[c], values.at[c], tm * frames
        else:
            b = 1 - tm if half == "outer" else half
            way = 0 if half == "outer" else half
            key, value = ext_k.at[i], ext_v.at[i]
            first = tm * frames + b * block - side
            for own, near, ext in ((keys, near_k, key), (values, near_v, value)):
                if half == "outer":
                    ext[pl.ds(pl.multiple_of(tm * side, side), 3 * side), :] = own[
                        c, pl.ds(pl.multiple_of((1 - tm) * side, side), 3 * side), :
                    ]
                    ext[pl.ds(pl.multiple_of((1 - tm) * 3 * side, side), side), :] = near[way, c]
                else:
                    ext[(1 - b) * side : (1 - b) * side + 3 * side, :] = own[c, b * side : b * side + 3 * side, :]
                    ext[b * 3 * side : b * 3 * side + side, :] = near[way, c]
        key_pos = first + lax.broadcasted_iota(jnp.int32, (block, span), 1)
        query_pos = tm * frames + b * block + lax.broadcasted_iota(jnp.int32, (block, span), 0)
        distance = jnp.abs(query_pos - key_pos)
        length, window = info[0, c, 0:1, :], info[1, c, 0:1, :]
        allowed = (distance <= window) & ((key_pos < length) | (distance == 0))
        if two_sided:
            allowed = allowed & (key_pos >= 0) & (key_pos < last)
        allowed = jnp.concatenate([allowed, allowed], axis=0)
        rows = pl.ds(pl.multiple_of(b * block, block), block)
        units += [(i, c, rows, key, value, allowed, cols) for cols in columns]
    size = STAGED * len(columns)
    for at in range(0, len(units), size):
        some = units[at : at + size]
        scores = [
            dot_nt(split_heads(queries[c, rows, cols], HS**-0.5), key[:, cols])
            for i, c, rows, key, value, allowed, cols in some
        ]
        scores = [jnp.where(unit[5], s, NEG_LARGE) for s, unit in zip(scores, some)]
        highest = [jnp.max(s, axis=1, keepdims=True) for s in scores]
        rising = [jnp.exp(s - peak).astype(BF16) for s, peak in zip(scores, highest)]
        mixes = [
            dot_f32(r, jnp.concatenate([value[:, cols], ones], axis=1))
            for r, (i, c, rows, key, value, allowed, cols) in zip(rising, some)
        ]
        for mix, unit in zip(mixes, some):
            top = jnp.where(lane < HS, mix[:block, :LANES], mix[block:, :LANES])
            total = jnp.where(lane < HS, mix[:block, LANES:], mix[block:, LANES:])
            out[unit[0], :, unit[6]] = (top / total).astype(BF16)


def project(flat, weight, out):
    clips, frames, width = out.shape
    chunk = 2 * LANES
    for at in range(0, width, chunk):
        part = dot_f32(flat, weight[:, at : at + chunk]).astype(BF16)
        out[:, :, at : at + chunk] = part.reshape(clips, frames, chunk)


def values_kernel(audio, wv, values):
    clips, frames, width = audio.shape
    project(audio[...].reshape(clips * frames, width), wv, values)


def make_values(audio, wv):
    return pl.pallas_call(
        values_kernel,
        name="values",
        out_shape=VMEM(audio.shape, BF16),
        in_specs=whole(2),
        out_specs=pl.BlockSpec(memory_space=VMEM),
        compiler_params=params(16),
        cost_estimate=cost(600_000_000, 2_000_000),
    )(audio, wv)


def queries_kernel(two_sided, tasks, info, audio, keys, values, wq, queries, done):
    clips, frames, width = audio.shape
    project(audio[...].reshape(clips * frames, width), wq, queries)
    attend(two_sided, tasks, info, queries, keys, values, None, None, None, None, done)


def context_of(tasks, frames, width):
    return VMEM((max(len(tasks), 1), frames // 2, width), BF16)


def make_queries(two_sided, tasks, info, audio, keys, values, wq):
    clips, frames, width = audio.shape
    return pl.pallas_call(
        functools.partial(queries_kernel, two_sided, tasks),
        name="queries",
        out_shape=[VMEM(audio.shape, BF16), context_of(tasks, frames, width)],
        in_specs=whole(5),
        out_specs=whole(2),
        compiler_params=params(16),
        cost_estimate=cost(80_000_000_000, 3_000_000, 100_000),
    )(info, audio, keys, values, wq)


def inner_kernel(two_sided, tasks, info, queries, keys, values, done):
    attend(two_sided, tasks, info, queries, keys, values, None, None, None, None, done)


def inner(two_sided, tasks, info, queries, keys, values):
    clips, frames, width = queries.shape
    return pl.pallas_call(
        functools.partial(inner_kernel, two_sided, tasks),
        name="inner",
        out_shape=context_of(tasks, frames, width),
        in_specs=whole(4),
        out_specs=pl.BlockSpec(memory_space=VMEM),
        compiler_params=params(16),
        cost_estimate=cost(300_000_000, 2_000_000, 100_000),
    )(info, queries, keys, values)


def mix_kernel(
    two_sided, plan, info, queries, keys, values, near, wk, wv, audio, wout, *rest
):
    count = len(plan) - 1
    before = rest[:count]
    mixed, frame_sum, context, done, near_k, near_v, ext_k, ext_v = rest[count:]
    clips, frames, width = queries.shape
    sides, side = near.shape[0], near.shape[2]
    block = frames // 2
    chunk = 2 * LANES
    tm = lax.axis_index("tm")
    beyond = near[...].reshape(sides * clips * side, width)
    for weight, out in ((wk, near_k), (wv, near_v)):
        for at in range(0, width, chunk):
            part = dot_f32(beyond, weight[:, at : at + chunk]).astype(BF16)
            out[:, :, :, at : at + chunk] = part.reshape(sides, clips, side, chunk)
    attend(two_sided, plan[-1], info, queries, keys, values, near_k, near_v, ext_k, ext_v, done)
    for tasks, held in zip(plan, (*before, done)):
        for i, (c, half) in enumerate(tasks):
            b = tm if half == "inner" else 1 - tm if half == "outer" else half
            context[c, pl.ds(pl.multiple_of(b * block, block), block), :] = held[i]
    place = tm * frames + lax.broadcasted_iota(jnp.int32, (frames, 1), 0)
    flat = context[...].reshape(clips * frames, width)
    for at in range(0, width, chunk):
        cols = slice(at, at + chunk)
        part = dot_f32(flat, wout[:, cols]).reshape(clips, frames, chunk)
        part = (audio[:, :, cols].astype(F32) + part).astype(BF16)
        mixed[:, :, cols] = part
        for c in range(clips):
            kept = jnp.where(place < info[0, c, 0:1, 0:1], part[c].astype(F32), 0.0)
            frame_sum[c : c + 1, cols] = jnp.sum(kept, axis=0, keepdims=True)


def mix(two_sided, plan, info, queries, keys, values, near, wk, wv, audio, wout, before):
    clips, frames, width = queries.shape
    beyond = VMEM(near.shape, BF16)
    return pl.pallas_call(
        functools.partial(mix_kernel, two_sided, plan),
        name="mix",
        out_shape=[VMEM(audio.shape, BF16), VMEM((clips, width), F32)],
        in_specs=whole(9 + len(before)),
        out_specs=whole(2),
        scratch_shapes=[VMEM((clips, frames, width), BF16), context_of(plan[-1], frames, width)]
        + [beyond, beyond]
        + [VMEM((len(plan[-1]), frames, width), BF16)] * 2,
        compiler_params=params(32),
        cost_estimate=cost(2_000_000_000, 8_000_000, 400_000),
    )(info, queries, keys, values, near, wk, wv, audio, wout, *before)


def pool_kernel(peaks, spans, others, weights, values, wvideo, out):
    clips, frames, width = values.shape
    tokens = peaks.shape[2]
    core = lax.rem(lax.axis_index("batch"), 2)
    top = spans[...]
    for k in range(others.shape[0]):
        top = jnp.maximum(top, others[k])
    total = jnp.exp(spans[...] - top)
    for k in range(others.shape[0]):
        total = total + jnp.exp(others[k] - top)
    alpha = jnp.exp(peaks[...] - top) / (total * tokens)
    head = lax.broadcasted_iota(jnp.int32, (STAT_ROWS, tokens), 0)
    owner = lax.broadcasted_iota(jnp.int32, (STAT_ROWS, width), 0)
    lane_head = lax.broadcasted_iota(jnp.int32, (STAT_ROWS, width), 1) // HS
    spread = [
        jnp.concatenate([jnp.where(head == h, alpha[c], 0.0).astype(BF16) for h in range(HA)], axis=1)
        for c in range(clips)
    ]
    share = [dot_nt(spread[c], weights[c]) for c in range(clips)]
    high = [s.astype(BF16) for s in share]
    low = [(s - h.astype(F32)).astype(BF16) for s, h in zip(share, high)]
    heard = [dot_f32(jnp.concatenate([high[c], low[c]], axis=0), values[c]) for c in range(clips)]
    heard = [h[:STAT_ROWS] + h[STAT_ROWS:] for h in heard]
    pooled = jnp.concatenate(
        [jnp.sum(jnp.where(owner == lane_head, h, 0.0), axis=0, keepdims=True) for h in heard], axis=0
    )
    rows = jnp.concatenate(
        [jnp.where(core == 0, pooled, 0.0), jnp.where(core == 0, 0.0, pooled)], axis=0
    )
    high = rows.astype(BF16)
    low = (rows - high.astype(F32)).astype(BF16)
    both = dot_f32(jnp.concatenate([high, low], axis=0), wvideo[...])
    out[...] = both[: 2 * clips] + both[2 * clips :]


def pool(peaks, spans, others, weights, values, wvideo):
    clips, frames, width = values.shape
    return pl.pallas_call(
        pool_kernel,
        name="pool",
        out_shape=VMEM((2 * clips, wvideo.shape[1]), F32),
        in_specs=whole(6),
        out_specs=pl.BlockSpec(memory_space=VMEM),
        compiler_params=params(16),
        cost_estimate=cost(200_000_000, 2_000_000),
    )(peaks, spans, others, weights, values, wvideo)


def unit_rows(matrix):
    return matrix / jnp.sqrt(jnp.sum(matrix * matrix, axis=1, keepdims=True) + 1e-06)


def column_of(info, k):
    return jnp.concatenate([info[k, c, 0:1, 0:1] for c in range(info.shape[1])], axis=0)


def in_parts(x):
    high = x.astype(BF16)
    rest = x - high.astype(F32)
    middle = rest.astype(BF16)
    low = (rest - middle.astype(F32)).astype(BF16)
    return jnp.concatenate([high, middle, low], axis=0)


def audio_head_kernel(info, mine, other, waudio, out, parts):
    mean = ((mine[...] + other[...]) / column_of(info, 0).astype(F32)).astype(BF16)
    found = unit_rows(dot_f32(mean, waudio[...]))
    out[...] = found
    parts[...] = in_parts(found)


def audio_head(info, mine, other, waudio):
    clips, width = mine.shape[0], waudio.shape[1]
    return pl.pallas_call(
        audio_head_kernel,
        name="audio_head",
        out_shape=[jax.ShapeDtypeStruct((clips, width), F32), VMEM((3 * clips, width), BF16)],
        in_specs=whole(4),
        out_specs=whole(2),
        compiler_params=params(8),
        cost_estimate=cost(20_000_000, 1_200_000),
    )(info, mine, other, waudio)


def logits_kernel(masks, info, parts, held, logits, row_loss, video_embed, ordered):
    clips = logits.shape[0]
    total = held.shape[0]
    place = lax.axis_index("batch")
    core = lax.rem(place, 2)
    chip = lax.div(place, 2)
    rows = 2 * clips
    wide = held[...].astype(F32)
    for j, mask in enumerate(masks):
        at = pl.multiple_of((chip ^ mask) * rows, rows)
        ordered[pl.ds(at, rows), :] = wide[j * rows : (j + 1) * rows]
    own = unit_rows(wide[:rows])
    video_embed[...] = jnp.where(core == 0, own[:clips], own[clips:])
    wide = ordered[...]
    scale = LOGIT_SCALE / jnp.sqrt(jnp.sum(wide * wide, axis=1, keepdims=True) + 1e-06)
    square = lax.broadcasted_iota(jnp.int32, (total, total), 0) == lax.broadcasted_iota(
        jnp.int32, (total, total), 1
    )
    scale = jnp.sum(jnp.where(square, scale, 0.0), axis=0, keepdims=True)
    found = dot_nt(parts[...], wide.astype(BF16))
    found = found[:clips] + found[clips : 2 * clips] + found[2 * clips :]
    found = found * scale + LOGIT_BIAS
    logits[...] = found
    column = lax.broadcasted_iota(jnp.int32, found.shape, 1)
    signed = jnp.where(column == column_of(info, 2), -found, found)
    loss = jnp.maximum(signed, 0.0) + jnp.log1p(jnp.exp(-jnp.abs(signed)))
    loss = jnp.sum(loss, axis=1, keepdims=True)
    square = lax.broadcasted_iota(jnp.int32, (clips, clips), 0) == lax.broadcasted_iota(
        jnp.int32, (clips, clips), 1
    )
    row_loss[...] = jnp.sum(jnp.where(square, loss, 0.0), axis=0, keepdims=True)


def logits_and_loss(masks, info, parts, held):
    clips = info.shape[1]
    total, width = held.shape
    return pl.pallas_call(
        functools.partial(logits_kernel, masks),
        name="logits_and_loss",
        out_shape=[
            jax.ShapeDtypeStruct((clips, total), F32),
            jax.ShapeDtypeStruct((1, clips), F32),
            jax.ShapeDtypeStruct((clips, width), F32),
        ],
        in_specs=whole(3),
        out_specs=whole(3),
        scratch_shapes=[VMEM((total, width), F32)],
        compiler_params=params(8),
        cost_estimate=cost(20_000_000, 300_000),
    )(info, parts, held)


def others_on_tm(x):
    count = lax.axis_size("tm")
    return jnp.stack(
        [
            lax.ppermute(x, "tm", [(i, (i + shift) % count) for i in range(count)])
            for shift in range(1, count)
        ]
    )


def beside(send, operand, work, inputs):
    operand, inputs = lax.optimization_barrier((operand, inputs))
    moved = send(operand)
    return lax.optimization_barrier((moved, work(*inputs)))


def move(x, mask, flip=0):
    batch = lax.axis_size("batch")
    tm = lax.axis_size("tm")
    pairs = [(b * tm + t, (b ^ mask) * tm + (t ^ flip)) for b in range(batch) for t in range(tm)]
    return lax.ppermute(x, ("batch", "tm"), pairs)


def chip_masks(chips):
    top = chips // 2
    groups = [(top,)]
    while top > 1:
        step = 4 if top % 4 == 0 else 2
        top //= step
        groups.append((3 * top, top, 2 * top) if step == 4 else (top,))
    return groups


def per_device(
    audio, video, pair_ids, windows, lengths, w_qkv, w_out, w_query, w_audio_embed, w_video_embed
):
    clips = audio.shape[0]
    tm = lax.axis_size("tm")
    chips = lax.axis_size("batch") // 2
    two_sided = tm > 2
    if two_sided:
        plan = ((), (), tuple((c, half) for c in range(clips) for half in range(2)))
    else:
        inside = tuple((c, "inner") for c in range(clips))
        outside = tuple((c, "outer") for c in range(clips))
        plan = (inside[:1], inside[1:], outside)
    peaks, spans, info, weights, keys, held_audio, halo, wq, wk, wv = front(
        lengths, windows, pair_ids, audio, video, w_qkv, w_query, two_sided
    )

    def spread(halo):
        if not two_sided:
            return move(halo, 0, 1)
        upward = lax.ppermute(halo[0], "tm", [(i, i + 1) for i in range(tm - 1)])
        downward = lax.ppermute(halo[1], "tm", [(i + 1, i) for i in range(tm - 1)])
        return jnp.stack([upward, downward])

    near = spread(halo)
    others = others_on_tm(spans)
    values = make_values(held_audio, wv)
    queries, part_a = make_queries(two_sided, plan[0], info, held_audio, keys, values, wq)
    others, (queries, part_a) = lax.optimization_barrier((others, (queries, part_a)))
    found = pool(peaks, spans, others, weights, values, w_video_embed)
    local = (info, queries, keys, values)
    if plan[1]:
        moved, part_b = beside(
            lambda x: move(x, 1), found, lambda *held: inner(two_sided, plan[1], *held), local
        )
    else:
        moved, part_b = move(found, 1), part_a
    found = found + moved

    def share(x):
        return lax.psum(x, "tm") if two_sided else x + move(x, 1, 1)

    found, (audio_mixed, frame_sum) = beside(
        share,
        found,
        lambda *held: mix(two_sided, plan, *held[:9], held[9:]),
        (*local, near, wk, wv, held_audio, w_out, part_a, part_b),
    )
    held = found.astype(BF16)
    if two_sided:
        frame_sum = lax.psum(frame_sum, "tm")
        other_sum = jnp.zeros_like(frame_sum)
    else:
        other_sum = move(frame_sum, 0, 1)
    masks = [0]
    for group in chip_masks(chips):
        held = jnp.concatenate([held] + [move(held, 2 * m + (m > 1)) for m in group], axis=0)
        masks = masks + [mask ^ m for m in group for mask in masks]
    audio_embed, unit_audio = audio_head(info, frame_sum, other_sum, w_audio_embed)
    logits, row_loss, video_embed = logits_and_loss(masks, info, unit_audio, held)
    return (audio_mixed, audio_embed, video_embed, logits, row_loss.reshape(clips))


def solution(mesh):
    in_specs = (
        P("batch", "tm", None),
        P("batch", None, None),
        P("batch"),
        P("batch"),
        P("batch"),
        P(),
        P(),
        P(),
        P(),
        P(),
    )
    out_specs = (
        P("batch", "tm", None),
        P("batch", None),
        P("batch", None),
        P("batch", None),
        P("batch"),
    )
    return jax.shard_map(
        per_device, mesh=mesh, in_specs=in_specs, out_specs=out_specs, check_vma=False
    )
```

```python
import functools

import jax
import jax.numpy as jnp
from jax import lax
from jax.experimental import pallas as pl
from jax.experimental.pallas import tpu as pltpu
from jax.sharding import PartitionSpec as P

HA = 12
HS = 64
NEG_LARGE = -1e30
LOGIT_SCALE = 10.0
LOGIT_BIAS = -10.0
F32 = jnp.float32
BF16 = jnp.bfloat16
LANES = 128
STAT_ROWS = 16
STAGED = 3
NT = (((1,), (1,)), ((), ()))
VMEM = pltpu.VMEM
MIB = 1 << 20


def whole(count):
    return [pl.BlockSpec(memory_space=VMEM)] * count


def params(mib):
    return pltpu.CompilerParams(vmem_limit_bytes=mib * MIB)


def cost(flops, moved, exps=0):
    return pl.CostEstimate(flops=flops, bytes_accessed=moved, transcendentals=exps)


def dot_f32(a, b):
    return jnp.dot(a, b, preferred_element_type=F32)


def dot_nt(a, b):
    return lax.dot_general(a, b, NT, preferred_element_type=F32)


def split_heads(rows, scale):
    lane = lax.broadcasted_iota(jnp.int32, (1, LANES), 1)
    low = jnp.where(lane < HS, scale, 0.0).astype(BF16)
    high = jnp.where(lane < HS, 0.0, scale).astype(BF16)
    return jnp.concatenate([rows * low, rows * high], axis=0)


class Pieces:
    def __init__(self, src, dst, sem, pieces):
        rows = dst.shape[0] // pieces
        cuts = [pl.ds(k * rows, rows) for k in range(pieces)]
        self.copies = [pltpu.make_async_copy(src.at[cut], dst.at[cut], sem) for cut in cuts]

    def start(self):
        for copy in self.copies:
            copy.start()

    def wait(self):
        for copy in self.copies:
            copy.wait()


def load_all(pairs, sems):
    copies = [Pieces(src, dst, sems.at[i], pieces) for i, (src, dst, pieces) in enumerate(pairs)]
    for copy in copies:
        copy.start()
    return copies


def in_hbm(*arrays):
    return [pltpu.with_memory_space_constraint(x, pltpu.HBM) for x in arrays]


def from_hbm(count):
    return [pl.BlockSpec(memory_space=pltpu.HBM)] * count


def front_kernel(
    two_sided, lengths, windows, pair_ids, audio_in, video_in, w_qkv, w_query,
    peaks, spans, info, weights, keys, audio, halo, wq, wk, wv,
    small, ask_w, video, totals, sems,
):
    clips, frames, width = audio.shape
    tokens = video.shape[1]
    side = halo.shape[2]
    chunk = 2 * LANES
    cuts = [slice(at, at + chunk) for at in range(0, width, chunk)]
    count = iter(range(sems.shape[0]))

    def piece(src, dst, pieces=1):
        return Pieces(src, dst, sems.at[next(count)], pieces)

    def start(copies):
        for copy in copies:
            copy.start()

    def wait(copies):
        for copy in copies:
            copy.wait()

    ints = [piece(src, small.at[k]) for k, src in enumerate((lengths, windows, pair_ids))]
    of_audio = piece(audio_in, audio, 2)
    of_keys = [piece(w_qkv.at[:, width : 2 * width], wk, 2)]
    of_video = piece(video_in, video, 2)
    of_asking = [piece(w_query, ask_w, 2)]
    later = [piece(w_qkv.at[:, 2 * width : 3 * width], wv, 2), piece(w_qkv.at[:, 0:width], wq, 2)]
    if two_sided:
        later.append(piece(audio_in.at[:, frames - side : frames, :], halo.at[0]))
        later.append(piece(audio_in.at[:, 0:side, :], halo.at[1]))
    else:
        at = pl.multiple_of((1 - lax.axis_index("tm")) * (frames - side), side)
        later.append(piece(audio_in.at[:, pl.ds(at, side), :], halo.at[0]))

    def make_keys():
        of_audio.wait()
        flat = audio[...].reshape(clips * frames, width)
        wait(of_keys)
        for cut in cuts:
            keys[:, :, cut] = dot_f32(flat, wk[:, cut]).astype(BF16).reshape(clips, frames, chunk)

    start(ints + [of_audio] + of_keys)
    wait(ints)
    start([of_video] + of_asking)
    make_keys()
    start(later)
    for k in range(3):
        for c in range(clips):
            info[k, c] = jnp.full(info.shape[2:], small[k, c], jnp.int32)
    rest = (clips, STAT_ROWS - HA, tokens)
    peaks[:, HA:STAT_ROWS, :] = jnp.zeros(rest, F32)
    totals[:, HA:STAT_ROWS, :] = jnp.ones(rest, F32)
    place = lax.axis_index("tm") * frames + lax.broadcasted_iota(jnp.int32, (frames, 1), 0)
    of_video.wait()
    wait(of_asking)

    def meet(c, pair, rows):
        both = split_heads(rows, HS**-0.5)
        scores = dot_nt(keys[c, :, pair * LANES : (pair + 1) * LANES], both)
        scores = jnp.where(place < small[0, c], scores, NEG_LARGE)
        peak = jnp.max(scores, axis=0, keepdims=True)
        rising = jnp.exp(scores - peak)
        total = jnp.sum(rising, axis=0, keepdims=True)
        weights[c, :, pair * 2 * tokens : (pair + 1) * 2 * tokens] = rising.astype(BF16)
        for k in range(2):
            row = slice(2 * pair + k, 2 * pair + k + 1)
            peaks[c, row, :] = peak[:, k * tokens : (k + 1) * tokens]
            totals[c, row, :] = total[:, k * tokens : (k + 1) * tokens]

    def ask(c):
        return dot_f32(video[c], ask_w[...]).astype(BF16)

    ahead = ask(0)
    for c in range(clips):
        now = ahead
        if c + 1 < clips:
            ahead = ask(c + 1)
        for pair in range(HA // 2):
            meet(c, pair, now[:, pair * LANES : (pair + 1) * LANES])
    spans[...] = peaks[...] + jnp.log(totals[...])
    wait(later)


def front(lengths, windows, pair_ids, audio, video, w_qkv, w_query, two_sided):
    clips, frames, width = audio.shape
    tokens, depth = video.shape[1:]
    square = VMEM((width, width), BF16)
    sides = 2 if two_sided else 1
    stat = VMEM((clips, STAT_ROWS, tokens), F32)
    return pl.pallas_call(
        functools.partial(front_kernel, two_sided),
        name="front",
        out_shape=[
            stat,
            stat,
            VMEM((3, clips, 8, LANES), jnp.int32),
            VMEM((clips, frames, HA * tokens), BF16),
            VMEM((clips, frames, width), BF16),
            VMEM((clips, frames, width), BF16),
            VMEM((sides, clips, frames // 4, width), BF16),
            square,
            square,
            square,
        ],
        in_specs=from_hbm(7),
        out_specs=whole(10),
        scratch_shapes=[
            pltpu.SMEM((3, clips), jnp.int32),
            VMEM((depth, width), BF16),
            VMEM((clips, tokens, depth), BF16),
            stat,
            pltpu.SemaphoreType.DMA((7 + sides + 2 * (width // (2 * LANES)),)),
        ],
        compiler_params=params(24),
        cost_estimate=cost(2_000_000_000, 8_000_000, 800_000),
    )(*in_hbm(lengths, windows, pair_ids, audio, video, w_qkv, w_query))


def attend(two_sided, tasks, info, queries, keys, values, near_k, near_v, ext_k, ext_v, out):
    clips, frames, width = queries.shape
    side = frames // 4
    block = 2 * side
    span = 4 * side
    tm = lax.axis_index("tm")
    last = lax.axis_size("tm") * frames
    lane = lax.broadcasted_iota(jnp.int32, (block, LANES), 1)
    ones = jnp.ones((span, LANES), BF16)
    columns = [slice(pair * LANES, (pair + 1) * LANES) for pair in range(HA // 2)]
    units = []
    for i, (c, half) in enumerate(tasks):
        if half == "inner":
            b = tm
            key, value, first = keys.at[c], values.at[c], tm * frames
        else:
            b = 1 - tm if half == "outer" else half
            way = 0 if half == "outer" else half
            key, value = ext_k.at[i], ext_v.at[i]
            first = tm * frames + b * block - side
            for own, near, ext in ((keys, near_k, key), (values, near_v, value)):
                if half == "outer":
                    ext[pl.ds(pl.multiple_of(tm * side, side), 3 * side), :] = own[
                        c, pl.ds(pl.multiple_of((1 - tm) * side, side), 3 * side), :
                    ]
                    ext[pl.ds(pl.multiple_of((1 - tm) * 3 * side, side), side), :] = near[way, c]
                else:
                    ext[(1 - b) * side : (1 - b) * side + 3 * side, :] = own[c, b * side : b * side + 3 * side, :]
                    ext[b * 3 * side : b * 3 * side + side, :] = near[way, c]
        key_pos = first + lax.broadcasted_iota(jnp.int32, (block, span), 1)
        query_pos = tm * frames + b * block + lax.broadcasted_iota(jnp.int32, (block, span), 0)
        distance = jnp.abs(query_pos - key_pos)
        length, window = info[0, c, 0:1, :], info[1, c, 0:1, :]
        allowed = (distance <= window) & ((key_pos < length) | (distance == 0))
        if two_sided:
            allowed = allowed & (key_pos >= 0) & (key_pos < last)
        allowed = jnp.concatenate([allowed, allowed], axis=0)
        rows = pl.ds(pl.multiple_of(b * block, block), block)
        units += [(i, c, rows, key, value, allowed, cols) for cols in columns]
    size = STAGED * len(columns)
    for at in range(0, len(units), size):
        some = units[at : at + size]
        scores = [
            dot_nt(split_heads(queries[c, rows, cols], HS**-0.5), key[:, cols])
            for i, c, rows, key, value, allowed, cols in some
        ]
        scores = [jnp.where(unit[5], s, NEG_LARGE) for s, unit in zip(scores, some)]
        highest = [jnp.max(s, axis=1, keepdims=True) for s in scores]
        rising = [jnp.exp(s - peak).astype(BF16) for s, peak in zip(scores, highest)]
        mixes = [
            dot_f32(r, jnp.concatenate([value[:, cols], ones], axis=1))
            for r, (i, c, rows, key, value, allowed, cols) in zip(rising, some)
        ]
        for mix, unit in zip(mixes, some):
            top = jnp.where(lane < HS, mix[:block, :LANES], mix[block:, :LANES])
            total = jnp.where(lane < HS, mix[:block, LANES:], mix[block:, LANES:])
            out[unit[0], :, unit[6]] = (top / total).astype(BF16)


def project(flat, weight, out):
    clips, frames, width = out.shape
    chunk = 2 * LANES
    for at in range(0, width, chunk):
        part = dot_f32(flat, weight[:, at : at + chunk]).astype(BF16)
        out[:, :, at : at + chunk] = part.reshape(clips, frames, chunk)


def values_kernel(audio, wv, values):
    clips, frames, width = audio.shape
    project(audio[...].reshape(clips * frames, width), wv, values)


def make_values(audio, wv):
    return pl.pallas_call(
        values_kernel,
        name="values",
        out_shape=VMEM(audio.shape, BF16),
        in_specs=whole(2),
        out_specs=pl.BlockSpec(memory_space=VMEM),
        compiler_params=params(16),
        cost_estimate=cost(600_000_000, 2_000_000),
    )(audio, wv)


def queries_kernel(two_sided, tasks, info, audio, keys, values, wq, queries, done):
    clips, frames, width = audio.shape
    project(audio[...].reshape(clips * frames, width), wq, queries)
    attend(two_sided, tasks, info, queries, keys, values, None, None, None, None, done)


def context_of(tasks, frames, width):
    return VMEM((max(len(tasks), 1), frames // 2, width), BF16)


def make_queries(two_sided, tasks, info, audio, keys, values, wq):
    clips, frames, width = audio.shape
    return pl.pallas_call(
        functools.partial(queries_kernel, two_sided, tasks),
        name="queries",
        out_shape=[VMEM(audio.shape, BF16), context_of(tasks, frames, width)],
        in_specs=whole(5),
        out_specs=whole(2),
        compiler_params=params(16),
        cost_estimate=cost(80_000_000_000, 3_000_000, 100_000),
    )(info, audio, keys, values, wq)


def inner_kernel(two_sided, tasks, info, queries, keys, values, done):
    attend(two_sided, tasks, info, queries, keys, values, None, None, None, None, done)


def inner(two_sided, tasks, info, queries, keys, values):
    clips, frames, width = queries.shape
    return pl.pallas_call(
        functools.partial(inner_kernel, two_sided, tasks),
        name="inner",
        out_shape=context_of(tasks, frames, width),
        in_specs=whole(4),
        out_specs=pl.BlockSpec(memory_space=VMEM),
        compiler_params=params(16),
        cost_estimate=cost(300_000_000, 2_000_000, 100_000),
    )(info, queries, keys, values)


def mix_kernel(
    two_sided, plan, info, queries, keys, values, near, wk, wv, audio, wout, *rest
):
    count = len(plan) - 1
    before = rest[:count]
    mixed, frame_sum, context, done, near_k, near_v, ext_k, ext_v = rest[count:]
    clips, frames, width = queries.shape
    sides, side = near.shape[0], near.shape[2]
    block = frames // 2
    chunk = 2 * LANES
    tm = lax.axis_index("tm")
    beyond = near[...].reshape(sides * clips * side, width)
    for weight, out in ((wk, near_k), (wv, near_v)):
        for at in range(0, width, chunk):
            part = dot_f32(beyond, weight[:, at : at + chunk]).astype(BF16)
            out[:, :, :, at : at + chunk] = part.reshape(sides, clips, side, chunk)
    attend(two_sided, plan[-1], info, queries, keys, values, near_k, near_v, ext_k, ext_v, done)
    for tasks, held in zip(plan, (*before, done)):
        for i, (c, half) in enumerate(tasks):
            b = tm if half == "inner" else 1 - tm if half == "outer" else half
            context[c, pl.ds(pl.multiple_of(b * block, block), block), :] = held[i]
    place = tm * frames + lax.broadcasted_iota(jnp.int32, (frames, 1), 0)
    flat = context[...].reshape(clips * frames, width)
    for at in range(0, width, chunk):
        cols = slice(at, at + chunk)
        part = dot_f32(flat, wout[:, cols]).reshape(clips, frames, chunk)
        part = (audio[:, :, cols].astype(F32) + part).astype(BF16)
        mixed[:, :, cols] = part
        for c in range(clips):
            kept = jnp.where(place < info[0, c, 0:1, 0:1], part[c].astype(F32), 0.0)
            frame_sum[c : c + 1, cols] = jnp.sum(kept, axis=0, keepdims=True)


def mix(two_sided, plan, info, queries, keys, values, near, wk, wv, audio, wout, before):
    clips, frames, width = queries.shape
    beyond = VMEM(near.shape, BF16)
    return pl.pallas_call(
        functools.partial(mix_kernel, two_sided, plan),
        name="mix",
        out_shape=[VMEM(audio.shape, BF16), VMEM((clips, width), F32)],
        in_specs=whole(9 + len(before)),
        out_specs=whole(2),
        scratch_shapes=[VMEM((clips, frames, width), BF16), context_of(plan[-1], frames, width)]
        + [beyond, beyond]
        + [VMEM((len(plan[-1]), frames, width), BF16)] * 2,
        compiler_params=params(32),
        cost_estimate=cost(2_000_000_000, 8_000_000, 400_000),
    )(info, queries, keys, values, near, wk, wv, audio, wout, *before)


def pool_kernel(peaks, spans, others, weights, values, wvideo, out):
    clips, frames, width = values.shape
    tokens = peaks.shape[2]
    core = lax.rem(lax.axis_index("batch"), 2)
    top = spans[...]
    for k in range(others.shape[0]):
        top = jnp.maximum(top, others[k])
    total = jnp.exp(spans[...] - top)
    for k in range(others.shape[0]):
        total = total + jnp.exp(others[k] - top)
    alpha = jnp.exp(peaks[...] - top) / (total * tokens)
    head = lax.broadcasted_iota(jnp.int32, (STAT_ROWS, tokens), 0)
    owner = lax.broadcasted_iota(jnp.int32, (STAT_ROWS, width), 0)
    lane_head = lax.broadcasted_iota(jnp.int32, (STAT_ROWS, width), 1) // HS
    spread = [
        jnp.concatenate([jnp.where(head == h, alpha[c], 0.0).astype(BF16) for h in range(HA)], axis=1)
        for c in range(clips)
    ]
    share = [dot_nt(spread[c], weights[c]) for c in range(clips)]
    high = [s.astype(BF16) for s in share]
    low = [(s - h.astype(F32)).astype(BF16) for s, h in zip(share, high)]
    heard = [dot_f32(jnp.concatenate([high[c], low[c]], axis=0), values[c]) for c in range(clips)]
    heard = [h[:STAT_ROWS] + h[STAT_ROWS:] for h in heard]
    pooled = jnp.concatenate(
        [jnp.sum(jnp.where(owner == lane_head, h, 0.0), axis=0, keepdims=True) for h in heard], axis=0
    )
    rows = jnp.concatenate(
        [jnp.where(core == 0, pooled, 0.0), jnp.where(core == 0, 0.0, pooled)], axis=0
    )
    high = rows.astype(BF16)
    low = (rows - high.astype(F32)).astype(BF16)
    both = dot_f32(jnp.concatenate([high, low], axis=0), wvideo[...])
    out[...] = both[: 2 * clips] + both[2 * clips :]


def pool(peaks, spans, others, weights, values, wvideo):
    clips, frames, width = values.shape
    return pl.pallas_call(
        pool_kernel,
        name="pool",
        out_shape=VMEM((2 * clips, wvideo.shape[1]), F32),
        in_specs=whole(6),
        out_specs=pl.BlockSpec(memory_space=VMEM),
        compiler_params=params(16),
        cost_estimate=cost(200_000_000, 2_000_000),
    )(peaks, spans, others, weights, values, wvideo)


def unit_rows(matrix):
    return matrix / jnp.sqrt(jnp.sum(matrix * matrix, axis=1, keepdims=True) + 1e-06)


def column_of(info, k):
    return jnp.concatenate([info[k, c, 0:1, 0:1] for c in range(info.shape[1])], axis=0)


def in_parts(x):
    high = x.astype(BF16)
    rest = x - high.astype(F32)
    middle = rest.astype(BF16)
    low = (rest - middle.astype(F32)).astype(BF16)
    return jnp.concatenate([high, middle, low, jnp.zeros_like(low)], axis=0)


def audio_head_kernel(info, mine, other, waudio, out, parts):
    mean = ((mine[...] + other[...]) / column_of(info, 0).astype(F32)).astype(BF16)
    found = unit_rows(dot_f32(mean, waudio[...]))
    out[...] = found
    parts[...] = in_parts(found)


def audio_head(info, mine, other, waudio):
    clips, width = mine.shape[0], waudio.shape[1]
    return pl.pallas_call(
        audio_head_kernel,
        name="audio_head",
        out_shape=[jax.ShapeDtypeStruct((clips, width), F32), VMEM((4 * clips, width), BF16)],
        in_specs=whole(4),
        out_specs=whole(2),
        compiler_params=params(8),
        cost_estimate=cost(20_000_000, 1_200_000),
    )(info, mine, other, waudio)


def logits_kernel(masks, info, parts, held, logits, row_loss, video_embed, ordered):
    clips = logits.shape[0]
    total = held.shape[0]
    place = lax.axis_index("batch")
    core = lax.rem(place, 2)
    chip = lax.div(place, 2)
    rows = 2 * clips
    wide = held[...].astype(F32)
    for j, mask in enumerate(masks):
        at = pl.multiple_of((chip ^ mask) * rows, rows)
        ordered[pl.ds(at, rows), :] = wide[j * rows : (j + 1) * rows]
    own = unit_rows(wide[:rows])
    video_embed[...] = jnp.where(core == 0, own[:clips], own[clips:])
    wide = ordered[...]
    scale = LOGIT_SCALE / jnp.sqrt(jnp.sum(wide * wide, axis=1, keepdims=True) + 1e-06)
    square = lax.broadcasted_iota(jnp.int32, (total, total), 0) == lax.broadcasted_iota(
        jnp.int32, (total, total), 1
    )
    scale = jnp.sum(jnp.where(square, scale, 0.0), axis=0, keepdims=True)
    found = dot_nt(parts[...], wide.astype(BF16))
    found = found[:clips] + found[clips : 2 * clips] + found[2 * clips : 3 * clips]
    found = found * scale + LOGIT_BIAS
    logits[...] = found
    column = lax.broadcasted_iota(jnp.int32, found.shape, 1)
    signed = jnp.where(column == column_of(info, 2), -found, found)
    loss = jnp.maximum(signed, 0.0) + jnp.log1p(jnp.exp(-jnp.abs(signed)))
    loss = jnp.sum(loss, axis=1, keepdims=True)
    square = lax.broadcasted_iota(jnp.int32, (clips, clips), 0) == lax.broadcasted_iota(
        jnp.int32, (clips, clips), 1
    )
    row_loss[...] = jnp.sum(jnp.where(square, loss, 0.0), axis=0, keepdims=True)


def logits_and_loss(masks, info, parts, held):
    clips = info.shape[1]
    total, width = held.shape
    return pl.pallas_call(
        functools.partial(logits_kernel, masks),
        name="logits_and_loss",
        out_shape=[
            jax.ShapeDtypeStruct((clips, total), F32),
            jax.ShapeDtypeStruct((1, clips), F32),
            jax.ShapeDtypeStruct((clips, width), F32),
        ],
        in_specs=whole(3),
        out_specs=whole(3),
        scratch_shapes=[VMEM((total, width), F32)],
        compiler_params=params(8),
        cost_estimate=cost(20_000_000, 300_000),
    )(info, parts, held)


def others_on_tm(x):
    count = lax.axis_size("tm")
    return jnp.stack(
        [
            lax.ppermute(x, "tm", [(i, (i + shift) % count) for i in range(count)])
            for shift in range(1, count)
        ]
    )


def beside(send, operand, work, inputs):
    operand, inputs = lax.optimization_barrier((operand, inputs))
    moved = send(operand)
    return lax.optimization_barrier((moved, work(*inputs)))


def move(x, mask, flip=0):
    batch = lax.axis_size("batch")
    tm = lax.axis_size("tm")
    pairs = [(b * tm + t, (b ^ mask) * tm + (t ^ flip)) for b in range(batch) for t in range(tm)]
    return lax.ppermute(x, ("batch", "tm"), pairs)


def chip_masks(chips):
    top = chips // 2
    groups = [(top,)]
    while top > 1:
        step = 4 if top % 4 == 0 else 2
        top //= step
        groups.append((3 * top, top, 2 * top) if step == 4 else (top,))
    return groups


def per_device(
    audio, video, pair_ids, windows, lengths, w_qkv, w_out, w_query, w_audio_embed, w_video_embed
):
    clips = audio.shape[0]
    tm = lax.axis_size("tm")
    chips = lax.axis_size("batch") // 2
    two_sided = tm > 2
    if two_sided:
        plan = ((), (), tuple((c, half) for c in range(clips) for half in range(2)))
    else:
        inside = tuple((c, "inner") for c in range(clips))
        outside = tuple((c, "outer") for c in range(clips))
        plan = (inside[:1], inside[1:], outside)
    peaks, spans, info, weights, keys, held_audio, halo, wq, wk, wv = front(
        lengths, windows, pair_ids, audio, video, w_qkv, w_query, two_sided
    )

    def spread(halo):
        if not two_sided:
            return move(halo, 0, 1)
        upward = lax.ppermute(halo[0], "tm", [(i, i + 1) for i in range(tm - 1)])
        downward = lax.ppermute(halo[1], "tm", [(i + 1, i) for i in range(tm - 1)])
        return jnp.stack([upward, downward])

    near = spread(halo)
    others = others_on_tm(spans)
    values = make_values(held_audio, wv)
    queries, part_a = make_queries(two_sided, plan[0], info, held_audio, keys, values, wq)
    others, (queries, part_a) = lax.optimization_barrier((others, (queries, part_a)))
    found = pool(peaks, spans, others, weights, values, w_video_embed)
    local = (info, queries, keys, values)
    if plan[1]:
        moved, part_b = beside(
            lambda x: move(x, 1), found, lambda *held: inner(two_sided, plan[1], *held), local
        )
    else:
        moved, part_b = move(found, 1), part_a
    found = found + moved

    def share(x):
        return lax.psum(x, "tm") if two_sided else x + move(x, 1, 1)

    found, (audio_mixed, frame_sum) = beside(
        share,
        found,
        lambda *held: mix(two_sided, plan, *held[:9], held[9:]),
        (*local, near, wk, wv, held_audio, w_out, part_a, part_b),
    )
    held = found.astype(BF16)
    if two_sided:
        frame_sum = lax.psum(frame_sum, "tm")
        other_sum = jnp.zeros_like(frame_sum)
    else:
        other_sum = move(frame_sum, 0, 1)
    masks = [0]
    for group in chip_masks(chips):
        held = jnp.concatenate([held] + [move(held, 2 * m + (m > 1)) for m in group], axis=0)
        masks = masks + [mask ^ m for m in group for mask in masks]
    audio_embed, unit_audio = audio_head(info, frame_sum, other_sum, w_audio_embed)
    logits, row_loss, video_embed = logits_and_loss(masks, info, unit_audio, held)
    return (audio_mixed, audio_embed, video_embed, logits, row_loss.reshape(clips))


def solution(mesh):
    in_specs = (
        P("batch", "tm", None),
        P("batch", None, None),
        P("batch"),
        P("batch"),
        P("batch"),
        P(),
        P(),
        P(),
        P(),
        P(),
    )
    out_specs = (
        P("batch", "tm", None),
        P("batch", None),
        P("batch", None),
        P("batch", None),
        P("batch"),
    )
    return jax.shard_map(
        per_device, mesh=mesh, in_specs=in_specs, out_specs=out_specs, check_vma=False
    )
```
